256 devices in a mesh: outer: 16 (over y_lo, x, core), node: 16 (over y_hi, z).
Axes of the slice: x: 4, y: 4 (y_hi: 2, y_lo: 2; y = y_hi * 2 + y_lo), z: 8, core: 2. Of those that a mesh axis runs over, the one named last changes fastest.
Arguments:
- tokens: bfloat16 [65536, 14848], P(('outer', 'node')), may hold values from -24 to 24
- cotangent: bfloat16 [65536, 256], P(('outer', 'node')), may hold values from -0.0234375 to 0.0234375
- weight_codes: bfloat16 [14848, 256], P('node'), may hold values from -127 to 127, as said below
- weight_scales: float32 [14848, 2], P('node'), may hold values from 4.103326e-05 to 0.00024619958
- weight_bits: int32 [256], replicated, may hold values 0 or 1
- grad_bits: int32 [256], replicated, may hold values 0 or 1
Outputs:
- output: bfloat16 [65536, 256], P(('outer', 'node'))
- grad_rotated: float32 [14848, 256], P(('outer', 'node'))
The draws below stay inside these ranges and needn't reach their ends.
Inputs may be any that keep to these rules, and one draw needn't show every extreme that they name: `weight_codes`: whole numbers.
All inputs are finite; a program needn't handle non-finite values.
Results may differ from the reference program's by a relative error of at most 0.015.
Values may be sent and summed in bfloat16 or wider, within the bound.
A program may use at most 128 MiB of HBM per device.

```python
import math
import jax
import jax.numpy as jnp
import numpy as np
from jax import lax

D = 14848
SLAB = 256
TOKENS = 65536


def draw_weight_codes(key, part):
    key = jax.random.fold_in(key, 11)
    values = jax.random.randint(key, (D, SLAB), -127, 128)
    return values.astype(jnp.float32).astype(jnp.bfloat16)


def set_ends(entries, key, least, largest):
    spot = [jax.random.randint(jax.random.fold_in(key, axis), (), 0, length) for axis, length in enumerate(entries.shape)]
    main_axis = entries.shape.index(max(entries.shape))
    beside = spot[:main_axis] + [(spot[main_axis] + 1) % entries.shape[main_axis]] + spot[main_axis + 1:]
    return entries.at[tuple(spot)].set(least).at[tuple(beside)].set(largest)


def spiked(entries, rng, source, target, parts, factor):
    def block_of(axis_at):
        return (jnp.arange(entries.shape[axis_at]) // (entries.shape[axis_at] // parts)).reshape((-1,) + (1,) * (entries.ndim - 1 - axis_at))

    first = jax.random.permutation(rng, parts)[block_of(target)]
    far = (block_of(target) + parts // 2) % parts
    return jnp.where((block_of(source) == first) | (block_of(source) == far), factor * entries, entries)


def shard_levels(key, shape, pieces, low, top_value):
    gain = 1.0
    for axis_at, blocks in pieces:
        steps = jax.random.uniform(jax.random.fold_in(jax.random.fold_in(key, 6), axis_at), (blocks,), jnp.float32, low / len(pieces), top_value / len(pieces))
        gain = gain * jnp.repeat(jnp.exp(steps), shape[axis_at] // blocks).reshape((-1,) + (1,) * (len(shape) - 1 - axis_at))
    return gain


def noise(own_key, dims, deviation, reach, cuts=(), dtype=jnp.bfloat16):
    values = deviation * jax.random.normal(own_key, dims, jnp.float32)
    if cuts:
        values = values * shard_levels(own_key, dims, cuts, -0.22, 0.18)
    return jnp.clip(values, -reach, reach).astype(dtype)


def heavy_noise(rng, shape, scale, bound, split, heavy, kind=jnp.bfloat16):
    entries = scale * jax.random.normal(rng, shape, jnp.float32)
    if split:
        entries = entries * shard_levels(rng, shape, split, -0.22, 0.18)
    return jnp.clip(spiked(entries, jax.random.fold_in(rng, 3), *heavy), -bound, bound).astype(kind)


def setup_inputs(seed: int = 0) -> dict:
    seeds = jax.random.split(jax.random.key(seed), 7)
    tokens = heavy_noise(seeds[0], (TOKENS, D), 1.0, 24.0, ((0, 256),), (0, 1, 256, 6.0))
    cotangent = noise(seeds[1], (TOKENS, SLAB), (TOKENS ** -0.5), 0.0234375, ((0, 256),))
    weight_codes = draw_weight_codes(jax.random.fold_in(seeds[6], 71), 0)
    weight_scales = jnp.clip(jnp.exp(math.log(0.00024619958) - 1.7917595 * jax.random.uniform(seeds[3], (D, SLAB // 128), jnp.float32) ** shard_levels(seeds[3], (D, SLAB // 128), ((0, 16),), -0.2, 0.2)), 4.1033261368284e-05, 0.00024619958)
    weight_bits = set_ends((jax.random.randint(seeds[4], (SLAB,), 0, 2) < 1).astype(jnp.int32), jax.random.fold_in(seeds[4], 1), 0, 1)
    grad_bits = set_ends((jax.random.randint(seeds[5], (SLAB,), 0, 2) < 1).astype(jnp.int32), jax.random.fold_in(seeds[5], 1), 0, 1)
    return {"tokens": tokens, "cotangent": cotangent, "weight_codes": weight_codes, "weight_scales": weight_scales, "weight_bits": weight_bits, "grad_bits": grad_bits}


def sylvester():
    row_index = np.arange(128).reshape(128, 1)
    column_index = np.arange(128).reshape(1, 128)
    parity = np.zeros((128, 128))
    for level in range(7):
        parity = parity + row_index // 2 ** level % 2 * (column_index // 2 ** level % 2)
    return 1.0 - 2.0 * (parity % 2)

def rotate(values, bits):
    height, width = values.shape
    signs = (2 * bits - 1).astype(jnp.float32)
    table = jnp.asarray(sylvester(), jnp.float32) / math.sqrt(128.0)
    blocks = (values * signs).reshape(height, width // 128, 128)
    return jnp.einsum('rbi,ij->rbj', blocks, table, precision=lax.Precision.HIGHEST).reshape(height, width)

def dequantize(codes, scales):
    height, width = codes.shape
    blocks = codes.astype(jnp.float32).reshape(height, width // 128, 128)
    return (blocks * scales[:, :, None]).reshape(height, width)

def reference(tokens, cotangent, weight_codes, weight_scales, weight_bits, grad_bits):
    weight = rotate(dequantize(weight_codes, weight_scales), weight_bits).astype(jnp.bfloat16)
    output = jnp.dot(tokens, weight, preferred_element_type=jnp.float32).astype(jnp.bfloat16)
    grad = lax.dot_general(tokens, cotangent, (((0,), (0,)), ((), ())), preferred_element_type=jnp.float32)
    return (output, rotate(grad, grad_bits))
```

```python
import math

import jax
import jax.numpy as jnp
import numpy as np
from jax import lax
from jax.experimental import pallas as pl
from jax.experimental.pallas import tpu as pltpu
from jax.sharding import PartitionSpec as P

MESH = pl.DeviceIdType.MESH
SHARD = 928
BLOCK = 58
WIN = 1024
EDGE = 96
ROOT = 1.0 / math.sqrt(128.0)


def sylvester():
    row_index = np.arange(128).reshape(128, 1)
    column_index = np.arange(128).reshape(1, 128)
    parity = np.zeros((128, 128))
    for level in range(7):
        parity = parity + row_index // 2**level % 2 * (column_index // 2**level % 2)
    return 1.0 - 2.0 * (parity % 2)


def kernel(
    tokens, cot_in, codes, scales, wbits, gbits, table,
    out, grad,
    tok, cot, wts, gwin, part, s1, d1, r1, s2, d2, r2, s3, d3, acc, other,
    tok_loc, tok_ss, tok_rs, cot_sem, w_ss, w_rs, ss1, rs1, ss2, rs2, ss3, rs3, o_sem,
):
    o = lax.axis_index("outer")
    n = lax.axis_index("node")
    c = lax.rem(o, 2)
    x = lax.rem(o // 2, 4)
    ylo = o // 8
    yhi = n // 8
    z = lax.rem(n, 8)
    y = yhi * 2 + ylo
    odd = lax.rem(z + c, 2)

    def dev(cc, xx, yy, zz):
        xx, yy, zz = lax.rem(xx + 4, 4), lax.rem(yy + 4, 4), lax.rem(zz + 8, 8)
        return (lax.rem(yy, 2) * 8 + xx * 2 + cc, (yy // 2) * 8 + zz)

    mate = dev(1 - c, x, y, z)
    xp, xm = dev(c, x + 1, y, z), dev(c, x - 1, y, z)
    yp, ym = dev(c, x, y + 1, z), dev(c, x, y - 1, z)
    zp, zm = dev(c, x, y, z + 1), dev(c, x, y, z - 1)
    ypart = dev(c, x, 3 - y, z)

    zero = jnp.zeros((EDGE, 256), jnp.bfloat16)

    @pl.loop(0, 8)
    def _(i):
        wts[i, pl.ds(0, EDGE)] = zero
        wts[i, pl.ds(WIN - EDGE, EDGE)] = zero

    barrier = pltpu.get_barrier_semaphore()
    peers = [mate, xp, xm, yp, ym] + [dev(c, x, y, z + k) for k in range(1, 8)]
    for p in peers:
        pl.semaphore_signal(barrier, inc=1, device_id=p, device_id_type=MESH)

    def start_of(g):
        return pl.multiple_of(g * SHARD - 32 * lax.rem(g, 4), 128)

    def order(i):
        if isinstance(i, int):
            i = jnp.int32(i)
        first = lax.rem(ylo + i, 2) * 4 + lax.rem(x + 2, 4)
        second = ylo * 4 + lax.rem(x + 1 + i, 4)
        third = (1 - ylo) * 4 + lax.rem(x + 2 + i, 4)
        return jnp.where(i < 2, first, jnp.where(i < 5, second, third))

    def local_tok(gi):
        return pltpu.make_async_copy(
            tokens.at[:, pl.ds(start_of(2 * gi + c), WIN)],
            tok.at[gi, pl.ds(pl.multiple_of(c * 256, 256), 256)],
            tok_loc.at[gi],
        )

    def swap_tok(gi):
        return pltpu.make_async_remote_copy(
            src_ref=tokens.at[:, pl.ds(start_of(2 * gi + 1 - c), WIN)],
            dst_ref=tok.at[gi, pl.ds(pl.multiple_of(c * 256, 256), 256)],
            send_sem=tok_ss.at[gi],
            recv_sem=tok_rs.at[gi],
            device_id=mate,
            device_id_type=MESH,
        )

    cot_mine = cot.at[pl.ds(pl.multiple_of(c * 256, 256), 256)]
    local_cot = pltpu.make_async_copy(cot_in, cot_mine, cot_sem.at[0])
    swap_cot = pltpu.make_async_remote_copy(
        src_ref=cot_in, dst_ref=cot_mine, send_sem=cot_sem.at[1], recv_sem=cot_sem.at[2],
        device_id=mate, device_id_type=MESH,
    )
    local_cot.start()

    @pl.loop(0, 8)
    def _(i):
        local_tok(order(i)).start()

    gwin[pl.ds(WIN, EDGE)] = jnp.zeros((EDGE, 256), jnp.float32)
    acc[...] = jnp.zeros_like(acc)

    def shard(yy, zz):
        zz = lax.rem(zz + 8, 8)
        slot = yy * 4 + zz // 2
        return slot, wts.at[slot, pl.ds(pl.multiple_of(32 * lax.rem(zz, 4), 32), SHARD)]

    def push(yy, zz, to, k):
        slot, rows = shard(yy, zz)
        return pltpu.make_async_remote_copy(
            src_ref=rows, dst_ref=rows, send_sem=w_ss.at[k], recv_sem=w_rs.at[slot],
            device_id=to, device_id_type=MESH,
        )

    def arrived(yy, zz):
        push(yy, zz, zp, 0).wait_recv()

    def multiply(yy, zz):
        slot = yy * 4 + lax.rem(zz + 8, 8) // 2
        for half in range(2):
            rows = pl.ds(half * 256, 256)
            acc[rows] += jnp.dot(tok[slot, rows], wts[slot], preferred_element_type=jnp.float32)

    @pl.when(odd == 0)
    def _():
        signs = (2 * wbits[...] - 1).astype(jnp.bfloat16)
        slot = yhi * 4 + z // 2
        base = pl.multiple_of(32 * lax.rem(z, 4), 32)
        for lo in range(0, SHARD, 464):
            for b in range(2):
                cols = pl.ds(b * 128, 128)
                spun = jnp.dot(
                    codes[pl.ds(lo, 464), cols] * signs[:, b * 128:b * 128 + 128], table[...],
                    preferred_element_type=jnp.float32,
                )
                spun = spun * (scales[pl.ds(lo, 464), b:b + 1] * ROOT)
                wts[slot, pl.ds(base + lo, 464), cols] = spun.astype(jnp.bfloat16)

    pl.semaphore_wait(barrier, len(peers))

    swap_cot.start()

    @pl.when(odd == 0)
    def _():
        push(yhi, z, zp, 0).start()
        push(yhi, z, zm, 1).start()
        push(yhi, z, ypart, 2).start()

    @pl.loop(0, 8)
    def _(i):
        swap_tok(order(i)).start()

    local_cot.wait()
    swap_cot.wait_recv()

    def produce(i):
        gi = order(i)
        local_tok(gi).wait()
        swap_tok(gi).wait_recv()
        top = EDGE - 32 * lax.rem(2 * gi + c, 4)

        @pl.loop(0, 4)
        def _(k):
            cols = pl.ds(pl.multiple_of(k * 256, 256), 256)
            piece = lax.dot_general(
                tok[gi, :, cols], cot[...], (((0,), (0,)), ((), ())), preferred_element_type=jnp.float32
            )
            gwin[pl.ds(pl.multiple_of(top + k * 256, 32), 256)] = piece

        for s in range(16):
            for h in range(2):
                part[h, gi, s] = gwin[pl.ds(EDGE + BLOCK * s, 64), pl.ds(h * 128, 128)]

    def ring(level, h):
        along_x = (h == 0) == (level == 1)
        pos = x if along_x else y
        ends = (xp, xm) if along_x else (yp, ym)
        sent, got = (s1, d1) if level == 1 else (s2, d2)
        ssem, rsem = (ss1, rs1) if level == 1 else (ss2, rs2)
        total = r1 if level == 1 else r2

        def copy(way, m):
            return pltpu.make_async_remote_copy(
                src_ref=sent.at[h, way, m], dst_ref=got.at[h, way, m],
                send_sem=ssem.at[h, way, m], recv_sem=rsem.at[h, way, m],
                device_id=ends[way], device_id_type=MESH,
            )

        def read(dest, half, i):
            if level == 1 and h == 0:
                return part[0, half * 4 + dest, i]
            if level == 1:
                return part[1, lax.rem(dest, 2) * 4 + 2 * half + i // 8, (dest // 2) * 8 + lax.rem(i, 8)]
            if h == 0:
                return r1[0, lax.rem(dest, 2) * 16 + (dest // 2) * 8 + half * 4 + i]
            return r1[1, dest * 8 + half * 4 + i]

        count = 16 if level == 1 else 4

        def send(way, m):
            off = (2, 1, 1)[m] if way == 0 else (2, 3, 3)[m]
            dest = lax.rem(pos + off, 4)
            half = (0, 1, 0)[m] if way == 0 else (1, 0, 1)[m]
            if m == 2:
                copy(way, 0).wait_recv()

            @pl.loop(0, count)
            def _(i):
                value = read(dest, half, i)
                if m == 2:
                    value = value + got[h, way, 0, i].astype(jnp.float32)
                sent[h, way, m, i] = value.astype(jnp.bfloat16)

            copy(way, m).start()

        def finish():
            for half in range(2):
                a, b = ((0, 2), (1, 1)) if half == 0 else ((0, 1), (1, 2))
                copy(*b).wait_recv()
                copy(*a).wait_recv()

                @pl.loop(0, count)
                def _(i):
                    value = (
                        read(pos, half, i)
                        + got[(h,) + a + (i,)].astype(jnp.float32)
                        + got[(h,) + b + (i,)].astype(jnp.float32)
                    )
                    if level == 1:
                        r1[h, half * 16 + i] = value
                    else:
                        r2[half * 4 + i, h] = value

        def drain():
            for way in range(2):
                for m in range(3):
                    copy(way, m).wait_send()

        return send, finish, drain

    send_a, finish_a, drain_a = ring(1, 0)
    send_b, finish_b, drain_b = ring(1, 1)
    send_c, finish_c, drain_c = ring(2, 0)
    send_d, finish_d, drain_d = ring(2, 1)

    pl.loop(0, 2)(produce)
    send_a(0, 0)
    send_a(1, 0)
    pl.loop(2, 5)(produce)
    send_b(0, 0)
    send_b(1, 0)

    near, far = yhi, 1 - yhi

    @pl.when(odd == 0)
    def _():
        arrived(far, z)
        push(far, z, zp, 3).start()
        push(far, z, zm, 4).start()

    @pl.when(odd == 1)
    def _():
        arrived(near, z - 1)
        push(near, z - 1, zp, 0).start()
        arrived(near, z + 1)
        push(near, z + 1, zm, 1).start()

    pl.loop(5, 8)(produce)
    send_a(0, 1)
    send_a(1, 1)
    send_b(0, 1)
    send_b(1, 1)
    send_a(0, 2)
    send_a(1, 2)

    @pl.when(odd == 0)
    def _():
        multiply(near, z)
        multiply(far, z)

    @pl.when(odd == 1)
    def _():
        arrived(far, z - 1)
        push(far, z - 1, zp, 2).start()
        arrived(far, z + 1)
        push(far, z + 1, zm, 3).start()
        multiply(near, z - 1)
        multiply(near, z + 1)

    send_b(0, 2)
    send_b(1, 2)

    @pl.when(odd == 0)
    def _():
        arrived(near, z - 2)
        push(near, z - 2, zp, 5).start()
        arrived(near, z + 2)
        push(near, z + 2, zm, 6).start()

    finish_a()
    send_c(0, 0)
    send_c(1, 0)
    send_c(0, 1)
    send_c(1, 1)

    @pl.when(odd == 0)
    def _():
        arrived(far, z - 2)
        push(far, z - 2, zp, 7).start()
        arrived(far, z + 2)
        push(far, z + 2, zm, 8).start()
        multiply(near, z - 2)
        multiply(near, z + 2)

    @pl.when(odd == 1)
    def _():
        arrived(near, z - 3)
        push(near, z - 3, zp, 4).start()
        multiply(far, z - 1)
        multiply(far, z + 1)

    finish_b()
    send_d(0, 0)
    send_d(1, 0)
    send_d(0, 1)
    send_d(1, 1)
    send_c(0, 2)
    send_c(1, 2)
    finish_c()
    send_d(0, 2)
    send_d(1, 2)

    @pl.when(odd == 1)
    def _():
        arrived(far, z + 3)
        push(far, z + 3, zm, 5).start()
        arrived(near, z + 3)
        multiply(near, z - 3)
        multiply(near, z + 3)

    finish_d()

    def last(k):
        to = lax.rem(z + k, 8)
        return pltpu.make_async_remote_copy(
            src_ref=s3.at[to], dst_ref=d3.at[k - 1], send_sem=ss3.at[k - 1], recv_sem=rs3.at[k - 1],
            device_id=dev(c, x, y, z + k), device_id_type=MESH,
        )

    for i in range(8):
        s3[i] = r2[i].astype(jnp.bfloat16)
    for k in (4, 3, 5, 2, 6, 1, 7):
        last(k).start()

    @pl.when(odd == 0)
    def _():
        multiply(far, z - 2)
        multiply(far, z + 2)
        arrived(near, z + 4)
        multiply(near, z + 4)
        arrived(far, z + 4)
        multiply(far, z + 4)

    @pl.when(odd == 1)
    def _():
        arrived(far, z - 3)
        multiply(far, z - 3)
        multiply(far, z + 3)

    theirs = pl.ds(pl.multiple_of((1 - c) * 256, 256), 256)
    mine = pl.ds(pl.multiple_of(c * 256, 256), 256)
    swap_out = pltpu.make_async_remote_copy(
        src_ref=acc.at[theirs], dst_ref=other, send_sem=o_sem.at[0], recv_sem=o_sem.at[1],
        device_id=mate, device_id_type=MESH,
    )
    swap_out.start()

    for k in range(1, 8):
        last(k).wait_recv()
    gsigns = (2 * gbits[...] - 1).astype(jnp.float32)
    for h in range(2):
        value = r2[z, h]
        for k in range(1, 8):
            value = value + d3[k - 1, h].astype(jnp.float32)
        value = value * gsigns[:, h * 128:h * 128 + 128]
        spun = jnp.zeros((64, 128), jnp.float32)
        for _ in range(3):
            head = value.astype(jnp.bfloat16)
            spun = spun + jnp.dot(head, table[...], preferred_element_type=jnp.float32)
            value = value - head.astype(jnp.float32)
        grad[:, h * 128:h * 128 + 128] = (spun * ROOT)[:BLOCK]

    swap_out.wait_recv()
    out[...] = (acc[mine] + other[...]).astype(jnp.bfloat16)

    swap_out.wait_send()
    swap_cot.wait_send()

    @pl.loop(0, 8)
    def _(i):
        swap_tok(i).wait_send()

    drain_a()
    drain_b()
    drain_c()
    drain_d()
    for k in range(1, 8):
        last(k).wait_send()

    @pl.when(odd == 0)
    def _():
        for k in range(9):
            push(yhi, z, zp, k).wait_send()

    @pl.when(odd == 1)
    def _():
        for k in range(6):
            push(yhi, z + 1, zp, k).wait_send()


def on_device(tokens, cotangent, weight_codes, weight_scales, weight_bits, grad_bits):
    table = jnp.asarray(sylvester(), jnp.bfloat16)
    vmem = pl.BlockSpec(memory_space=pltpu.VMEM)
    hbm = pl.BlockSpec(memory_space=pl.ANY)
    dma = pltpu.SemaphoreType.DMA
    bf, f32 = jnp.bfloat16, jnp.float32
    return pl.pallas_call(
        kernel,
        out_shape=(
            jax.ShapeDtypeStruct((256, 256), bf),
            jax.ShapeDtypeStruct((BLOCK, 256), f32),
        ),
        in_specs=[hbm, hbm, vmem, vmem, vmem, vmem, vmem],
        out_specs=(vmem, vmem),
        scratch_shapes=[
            pltpu.VMEM((8, 512, WIN), bf),
            pltpu.VMEM((512, 256), bf),
            pltpu.VMEM((8, WIN, 256), bf),
            pltpu.VMEM((WIN + EDGE, 256), f32),
            pltpu.VMEM((2, 8, 16, 64, 128), f32),
            pltpu.VMEM((2, 2, 3, 16, 64, 128), bf),
            pltpu.VMEM((2, 2, 3, 16, 64, 128), bf),
            pltpu.VMEM((2, 32, 64, 128), f32),
            pltpu.VMEM((2, 2, 3, 4, 64, 128), bf),
            pltpu.VMEM((2, 2, 3, 4, 64, 128), bf),
            pltpu.VMEM((8, 2, 64, 128), f32),
            pltpu.VMEM((8, 2, 64, 128), bf),
            pltpu.VMEM((7, 2, 64, 128), bf),
            pltpu.VMEM((512, 256), f32),
            pltpu.VMEM((256, 256), f32),
            dma((8,)), dma((8,)), dma((8,)), dma((3,)), dma((9,)), dma((8,)),
            dma((2, 2, 3)), dma((2, 2, 3)), dma((2, 2, 3)), dma((2, 2, 3)),
            dma((7,)), dma((7,)), dma((2,)),
        ],
        compiler_params=pltpu.CompilerParams(
            collective_id=0, has_side_effects=True, vmem_limit_bytes=56 * 2**20
        ),
        cost_estimate=pl.CostEstimate(flops=4 * 10**9, bytes_accessed=10**7, transcendentals=0),
    )(
        tokens, cotangent, weight_codes, weight_scales,
        weight_bits.reshape(1, 256), grad_bits.reshape(1, 256), table,
    )


def solution(mesh):
    return jax.shard_map(
        on_device,
        mesh=mesh,
        in_specs=(
            P(("outer", "node"), None),
            P(("outer", "node"), None),
            P("node", None),
            P("node", None),
            P(),
            P(),
        ),
        out_specs=(P(("outer", "node"), None), P(("outer", "node"), None)),
        check_vma=False,
    )
```

```python
import math

import jax
import jax.numpy as jnp
import numpy as np
from jax import lax
from jax.experimental import pallas as pl
from jax.experimental.pallas import tpu as pltpu
from jax.sharding import PartitionSpec as P

MESH = pl.DeviceIdType.MESH
SHARD = 928
BLOCK = 58
WIN = 1024
EDGE = 96
HALF = SHARD // 2
END = 128
RUN = HALF - END
ROOT = 1.0 / math.sqrt(128.0)


def sylvester():
    row_index = np.arange(128).reshape(128, 1)
    column_index = np.arange(128).reshape(1, 128)
    parity = np.zeros((128, 128))
    for level in range(7):
        parity = parity + row_index // 2**level % 2 * (column_index // 2**level % 2)
    return 1.0 - 2.0 * (parity % 2)


def kernel(
    tokens, cot_in, codes, scales, wbits, gbits, table,
    out, grad,
    raw, tok, cot, wts, part, s1, d1, r1, s2, d2, r2, s3, d3, acc, other,
    tok_loc, tok_ss, tok_rs, cot_sem, w_ss, w_rs, e_ss, e_rs, ss1, rs1, ss2, rs2, ss3, rs3, o_sem,
):
    o = lax.axis_index("outer")
    n = lax.axis_index("node")
    c = lax.rem(o, 2)
    x = lax.rem(o // 2, 4)
    ylo = o // 8
    yhi = n // 8
    z = lax.rem(n, 8)
    y = yhi * 2 + ylo
    odd = lax.rem(z + c, 2)

    def dev(cc, xx, yy, zz):
        xx, yy, zz = lax.rem(xx + 4, 4), lax.rem(yy + 4, 4), lax.rem(zz + 8, 8)
        return (lax.rem(yy, 2) * 8 + xx * 2 + cc, (yy // 2) * 8 + zz)

    mate = dev(1 - c, x, y, z)
    xp, xm = dev(c, x + 1, y, z), dev(c, x - 1, y, z)
    yp, ym = dev(c, x, y + 1, z), dev(c, x, y - 1, z)
    zp, zm = dev(c, x, y, z + 1), dev(c, x, y, z - 1)
    ypart = dev(c, x, 3 - y, z)
    xodd = lax.rem(x, 2)
    xpair, ypair = dev(c, x + 1 - 2 * xodd, y, z), dev(c, x, y + 1 - 2 * ylo, z)

    zero = jnp.zeros((EDGE, 256), jnp.bfloat16)

    @pl.loop(0, 8)
    def _(i):
        wts[i, pl.ds(0, EDGE)] = zero
        wts[i, pl.ds(WIN - EDGE, EDGE)] = zero

    barrier = pltpu.get_barrier_semaphore()
    peers = [mate, xp, xm, yp, ym] + [dev(c, x, y, z + k) for k in range(1, 8)]
    for p in peers:
        pl.semaphore_signal(barrier, inc=1, device_id=p, device_id_type=MESH)

    def start_of(g):
        return pl.multiple_of(g * SHARD - 32 * lax.rem(g, 4), 128)

    def order(i):
        if isinstance(i, int):
            i = jnp.int32(i)
        first = lax.rem(ylo + i, 2) * 4 + lax.rem(x + 2, 4)
        second = ylo * 4 + lax.rem(x + 1 + i, 4)
        third = (1 - ylo) * 4 + lax.rem(x + 2 + i, 4)
        return jnp.where(i < 2, first, jnp.where(i < 5, second, third))

    def local_tok(gi):
        return pltpu.make_async_copy(
            tokens.at[:, pl.ds(start_of(2 * gi + c), WIN)],
            tok.at[gi, pl.ds(pl.multiple_of(c * 256, 256), 256)],
            tok_loc.at[gi],
        )

    def swap_tok(gi):
        return pltpu.make_async_remote_copy(
            src_ref=tokens.at[:, pl.ds(start_of(2 * gi + 1 - c), WIN)],
            dst_ref=tok.at[gi, pl.ds(pl.multiple_of(c * 256, 256), 256)],
            send_sem=tok_ss.at[gi],
            recv_sem=tok_rs.at[gi],
            device_id=mate,
            device_id_type=MESH,
        )

    cot_mine = cot.at[pl.ds(pl.multiple_of(c * 256, 256), 256)]
    local_cot = pltpu.make_async_copy(cot_in, cot_mine, cot_sem.at[0])
    swap_cot = pltpu.make_async_remote_copy(
        src_ref=cot_in, dst_ref=cot_mine, send_sem=cot_sem.at[1], recv_sem=cot_sem.at[2],
        device_id=mate, device_id_type=MESH,
    )
    local_codes = pltpu.make_async_copy(codes, raw, cot_sem.at[3])

    @pl.when(odd == 0)
    def _():
        local_codes.start()

    local_cot.start()

    @pl.loop(0, 8)
    def _(i):
        local_tok(order(i)).start()

    for h in range(2):
        for i in range(4):
            r1[h, i, pl.ds(HALF, 8)] = jnp.zeros((8, 128), jnp.float32)
    acc[...] = jnp.zeros_like(acc)

    def shard(yy, zz):
        zz = lax.rem(zz + 8, 8)
        slot = yy * 4 + zz // 2
        return slot, 32 * lax.rem(zz, 4)

    def rows_of(yy, zz, first, size):
        slot, base = shard(yy, zz)
        return wts.at[slot, pl.ds(pl.multiple_of(base + first, 16), size)]

    def move(ref, to, ss, rs):
        return pltpu.make_async_remote_copy(
            src_ref=ref, dst_ref=ref, send_sem=ss, recv_sem=rs, device_id=to, device_id_type=MESH
        )

    def push(yy, zz, to, k, i):
        slot, _ = shard(yy, zz)
        skip = (xodd, ylo)[i] * END
        return move(rows_of(yy, zz, i * HALF + skip, RUN), to, w_ss.at[k, i], w_rs.at[slot, i])

    def partner(yy, i):
        slot, _ = shard(yy, z)
        return move(rows_of(yy, z, i * HALF, HALF), ypart, w_ss.at[8, i], w_rs.at[slot, i])

    def swap_end(yy, zz, k, i):
        slot, _ = shard(yy, zz)
        own = (xodd, ylo)[i] * RUN
        return move(rows_of(yy, zz, i * HALF + own, END), (xpair, ypair)[i], e_ss.at[k, i], e_rs.at[slot, i])

    def passing(yy, zz, i, k, to=None, j=0):
        push(yy, zz, zp, 0, i).wait_recv()
        if to is not None:
            push(yy, zz, to, j, i).start()
        swap_end(yy, zz, k, i).start()

    def complete(yy, zz):
        for i in range(2):
            swap_end(yy, zz, 0, i).wait_recv()

    near, far = yhi, 1 - yhi

    def multiply(j):
        dz0 = jnp.where(j < 2, 0, jnp.where(j < 6, jnp.where(lax.rem(j, 2) == 0, -2, 2), 4))
        far0 = jnp.where((j == 1) | (j == 4) | (j == 5) | (j == 7), 1, 0)
        dz1 = jnp.where(j < 4, 1, 3) * jnp.where(lax.rem(j, 2) == 0, -1, 1)
        far1 = jnp.where(lax.rem(j, 4) < 2, 0, 1)
        dz = jnp.where(odd == 0, dz0, dz1)
        off = jnp.where(odd == 0, far0, far1)
        slot = lax.rem(yhi + off, 2) * 4 + lax.rem(z + dz + 8, 8) // 2
        for half in range(2):
            rows = pl.ds(half * 256, 256)
            acc[rows] += jnp.dot(tok[slot, rows], wts[slot], preferred_element_type=jnp.float32)

    @pl.when(odd == 0)
    def _():
        signs = (2 * wbits[...] - 1).astype(jnp.bfloat16)
        factors = (scales[...] * ROOT).T
        local_codes.wait()
        slot = yhi * 4 + z // 2
        base = pl.multiple_of(32 * lax.rem(z, 4), 32)
        for lo in range(0, SHARD, 464):
            for b in range(2):
                cols = pl.ds(b * 128, 128)
                spun = jnp.dot(
                    raw[pl.ds(lo, 464), cols] * signs[:, b * 128:b * 128 + 128], table[...],
                    preferred_element_type=jnp.float32,
                )
                spun = spun * factors[lo:lo + 464, b:b + 1]
                wts[slot, pl.ds(base + lo, 464), cols] = spun.astype(jnp.bfloat16)

    pl.semaphore_wait(barrier, len(peers))

    swap_cot.start()

    @pl.when(odd == 0)
    def _():
        for i in range(2):
            push(near, z, zp, 0, i).start()
            push(near, z, zm, 1, i).start()
            partner(near, i).start()

    @pl.loop(0, 8)
    def _(i):
        swap_tok(order(i)).start()

    local_cot.wait()
    swap_cot.wait_recv()

    def produce(i):
        gi = order(i)
        local_tok(gi).wait()
        swap_tok(gi).wait_recv()
        sums = lax.dot_general(
            tok[gi], cot[...], (((0,), (0,)), ((), ())), preferred_element_type=jnp.float32
        )
        part[0, gi] = sums[:, :128]
        part[1, gi] = sums[:, 128:]

    def ring(level, h):
        along_x = (h == 0) == (level == 1)
        pos = x if along_x else y
        ends = (xp, xm) if along_x else (yp, ym)
        sent, got = (s1, d1) if level == 1 else (s2, d2)
        ssem, rsem = (ss1, rs1) if level == 1 else (ss2, rs2)
        total = r1 if level == 1 else r2

        def copy(way, m):
            return pltpu.make_async_remote_copy(
                src_ref=sent.at[h, way, m], dst_ref=got.at[h, way, m],
                send_sem=ssem.at[h, way, m], recv_sem=rsem.at[h, way, m],
                device_id=ends[way], device_id_type=MESH,
            )

        count = 2 if level == 1 else 4

        def read(dest, half, i):
            if level == 1:
                gi = half * 4 + dest if h == 0 else lax.rem(dest, 2) * 4 + 2 * half + i
                top = 32 * lax.rem(2 * gi + c, 4) + (i if h == 0 else dest // 2) * HALF
                return part[h, gi, pl.ds(pl.multiple_of(top, 16), HALF)]
            block = lax.rem(dest, 2) * 2 + dest // 2 if h == 0 else dest
            return r1[h, block, pl.ds(BLOCK * (half * 4 + i), 64)]

        def send(way, m):
            off = (2, 1, 1)[m] if way == 0 else (2, 3, 3)[m]
            dest = lax.rem(pos + off, 4)
            half = (0, 1, 0)[m] if way == 0 else (1, 0, 1)[m]
            if m == 2:
                copy(way, 0).wait_recv()
            for i in range(count):
                value = read(dest, half, i)
                if m == 2:
                    value = value + got[h, way, 0, i].astype(jnp.float32)
                sent[h, way, m, i] = value.astype(jnp.bfloat16)
            copy(way, m).start()

        def finish():
            for half in range(2):
                a, b = ((0, 2), (1, 1)) if half == 0 else ((0, 1), (1, 2))
                copy(*b).wait_recv()
                copy(*a).wait_recv()
                for i in range(count):
                    value = (
                        read(pos, half, i)
                        + got[(h,) + a + (i,)].astype(jnp.float32)
                        + got[(h,) + b + (i,)].astype(jnp.float32)
                    )
                    if level == 1:
                        r1[h, half * 2 + i, pl.ds(0, HALF)] = value
                    else:
                        r2[half * 4 + i, h] = value

        def drain():
            for way in range(2):
                for m in range(3):
                    copy(way, m).wait_send()

        return send, finish, drain

    send_a, finish_a, drain_a = ring(1, 0)
    send_b, finish_b, drain_b = ring(1, 1)
    send_c, finish_c, drain_c = ring(2, 0)
    send_d, finish_d, drain_d = ring(2, 1)

    def last(h, k):
        to = lax.rem(z + k, 8)
        return pltpu.make_async_remote_copy(
            src_ref=s3.at[h, to], dst_ref=d3.at[h, k - 1],
            send_sem=ss3.at[h, k - 1], recv_sem=rs3.at[h, k - 1],
            device_id=dev(c, x, y, z + k), device_id_type=MESH,
        )

    def last_sends(h):
        for i in range(8):
            s3[h, i] = r2[i, h].astype(jnp.bfloat16)
        for k in (4, 3, 5, 2, 6, 1, 7):
            last(h, k).start()

    def far_own(i):
        partner(far, i).wait_recv()
        push(far, z, zp, 2, i).start()
        push(far, z, zm, 3, i).start()

    def even_near2(i):
        passing(near, z - 2, i, 0, zp, 4)
        passing(near, z + 2, i, 1, zm, 5)

    def even_far2(i):
        passing(far, z - 2, i, 2, zp, 6)
        passing(far, z + 2, i, 3, zm, 7)

    def odd_near1(i):
        passing(near, z - 1, i, 0, zp, 0)
        passing(near, z + 1, i, 1, zm, 1)

    def odd_far1(i):
        passing(far, z - 1, i, 2, zp, 2)
        passing(far, z + 1, i, 3, zm, 3)

    def odd_near3(i):
        passing(near, z - 3, i, 4, zp, 4)
        passing(near, z + 3, i, 5)

    def odd_far3(i):
        passing(far, z + 3, i, 7, zm, 5)
        passing(far, z - 3, i, 6)

    def both(yy, d):
        complete(yy, z - d)
        complete(yy, z + d)

    def ring_start(send, *ms):
        for m in ms:
            send(0, m)
            send(1, m)

    def product(first, last_one):
        pl.loop(first, last_one)(multiply)

    def run(who, act):
        if who == 2:
            act()
        else:
            pl.when(odd == who)(act)

    steps = [
        (2.5, 2, lambda: pl.loop(0, 2)(produce)),
        (2.6, 2, lambda: ring_start(send_a, 0)),
        (5.5, 2, lambda: pl.loop(2, 5)(produce)),
        (5.6, 2, lambda: ring_start(send_b, 0)),
        (8.6, 2, lambda: pl.loop(5, 8)(produce)),
        (8.7, 2, lambda: ring_start(send_a, 1)),
        (8.8, 2, lambda: ring_start(send_b, 1)),
        (10.5, 2, lambda: ring_start(send_a, 2)),
        (13.5, 2, lambda: ring_start(send_b, 2)),
        (21.0, 2, finish_a),
        (21.1, 2, lambda: ring_start(send_c, 0, 1)),
        (23.0, 2, finish_b),
        (23.1, 2, lambda: ring_start(send_d, 0, 1)),
        (24.0, 2, lambda: ring_start(send_c, 2)),
        (26.0, 2, lambda: ring_start(send_d, 2)),
        (26.5, 2, finish_c),
        (26.6, 2, lambda: last_sends(0)),
        (28.5, 2, finish_d),
        (28.6, 2, lambda: last_sends(1)),
        (12.0, 2, lambda: product(0, 2)),
        (17.0, 2, lambda: product(2, 4)),
        (25.0, 2, lambda: product(4, 6)),
        (36.0, 2, lambda: product(6, 8)),
        (4.0, 0, lambda: far_own(0)),
        (6.0, 0, lambda: far_own(1)),
        (8.0, 0, lambda: even_near2(0)),
        (10.0, 0, lambda: even_near2(1)),
        (12.1, 0, lambda: even_far2(0)),
        (14.0, 0, lambda: even_far2(1)),
        (16.9, 0, lambda: both(near, 2)),
        (19.0, 0, lambda: passing(near, z + 4, 0, 4)),
        (21.5, 0, lambda: passing(near, z + 4, 1, 4)),
        (24.9, 0, lambda: both(far, 2)),
        (25.5, 0, lambda: passing(far, z + 4, 0, 5)),
        (28.7, 0, lambda: passing(far, z + 4, 1, 5)),
        (35.8, 0, lambda: complete(near, z + 4)),
        (35.9, 0, lambda: complete(far, z + 4)),
        (3.3, 1, lambda: odd_near1(0)),
        (5.4, 1, lambda: odd_near1(1)),
        (7.0, 1, lambda: odd_far1(0)),
        (9.0, 1, lambda: odd_far1(1)),
        (11.9, 1, lambda: both(near, 1)),
        (14.1, 1, lambda: odd_near3(0)),
        (16.0, 1, lambda: odd_near3(1)),
        (16.9, 1, lambda: both(far, 1)),
        (20.0, 1, lambda: odd_far3(0)),
        (22.0, 1, lambda: odd_far3(1)),
        (24.9, 1, lambda: both(near, 3)),
        (35.9, 1, lambda: both(far, 3)),
    ]
    for _, who, act in sorted(steps, key=lambda step: step[0]):
        run(who, act)

    theirs = pl.ds(pl.multiple_of((1 - c) * 256, 256), 256)
    mine = pl.ds(pl.multiple_of(c * 256, 256), 256)
    swap_out = pltpu.make_async_remote_copy(
        src_ref=acc.at[theirs], dst_ref=other, send_sem=o_sem.at[0], recv_sem=o_sem.at[1],
        device_id=mate, device_id_type=MESH,
    )
    swap_out.start()

    gsigns = (2 * gbits[...] - 1).astype(jnp.float32)
    for h in range(2):
        value = r2[z, h]
        for k in range(1, 8):
            last(h, k).wait_recv()
            value = value + d3[h, k - 1].astype(jnp.float32)
        value = value * gsigns[:, h * 128:h * 128 + 128]
        spun = jnp.zeros((64, 128), jnp.float32)
        for _ in range(3):
            head = value.astype(jnp.bfloat16)
            spun = spun + jnp.dot(head, table[...], preferred_element_type=jnp.float32)
            value = value - head.astype(jnp.float32)
        grad[:, h * 128:h * 128 + 128] = (spun * ROOT)[:BLOCK]

    swap_out.wait_recv()
    out[...] = (acc[mine] + other[...]).astype(jnp.bfloat16)

    swap_out.wait_send()
    swap_cot.wait_send()

    @pl.loop(0, 8)
    def _(i):
        swap_tok(i).wait_send()

    drain_a()
    drain_b()
    drain_c()
    drain_d()
    for h in range(2):
        for k in range(1, 8):
            last(h, k).wait_send()

    def sent_all(pushes, ends):
        for i in range(2):
            for k in range(pushes):
                push(near, z + odd, zp, k, i).wait_send()
            for k in range(ends):
                swap_end(near, z + odd, k, i).wait_send()

    def sent_even():
        for i in range(2):
            partner(near, i).wait_send()
        sent_all(8, 6)

    run(0, sent_even)
    run(1, lambda: sent_all(6, 8))


def place(out_in, grad_in, out, grad):
    out[...] = out_in[...]
    grad[...] = grad_in[...]


def on_device(tokens, cotangent, weight_codes, weight_scales, weight_bits, grad_bits):
    table = jnp.asarray(sylvester(), jnp.bfloat16)
    vmem = pl.BlockSpec(memory_space=pltpu.VMEM)
    hbm = pl.BlockSpec(memory_space=pl.ANY)
    dma = pltpu.SemaphoreType.DMA
    bf, f32 = jnp.bfloat16, jnp.float32
    shapes = (jax.ShapeDtypeStruct((256, 256), bf), jax.ShapeDtypeStruct((BLOCK, 256), f32))
    raw = pl.pallas_call(
        kernel,
        out_shape=shapes,
        in_specs=[hbm, hbm, hbm, vmem, vmem, vmem, vmem],
        out_specs=(vmem, vmem),
        scratch_shapes=[
            pltpu.VMEM((SHARD, 256), bf),
            pltpu.VMEM((8, 512, WIN), bf),
            pltpu.VMEM((512, 256), bf),
            pltpu.VMEM((8, WIN, 256), bf),
            pltpu.VMEM((2, 8, WIN, 128), f32),
            pltpu.VMEM((2, 2, 3, 2, HALF, 128), bf),
            pltpu.VMEM((2, 2, 3, 2, HALF, 128), bf),
            pltpu.VMEM((2, 4, HALF + 8, 128), f32),
            pltpu.VMEM((2, 2, 3, 4, 64, 128), bf),
            pltpu.VMEM((2, 2, 3, 4, 64, 128), bf),
            pltpu.VMEM((8, 2, 64, 128), f32),
            pltpu.VMEM((2, 8, 64, 128), bf),
            pltpu.VMEM((2, 7, 64, 128), bf),
            pltpu.VMEM((512, 256), f32),
            pltpu.VMEM((256, 256), f32),
            dma((8,)), dma((8,)), dma((8,)), dma((4,)),
            dma((9, 2)), dma((8, 2)), dma((8, 2)), dma((8, 2)),
            dma((2, 2, 3)), dma((2, 2, 3)), dma((2, 2, 3)), dma((2, 2, 3)),
            dma((2, 7)), dma((2, 7)), dma((2,)),
        ],
        compiler_params=pltpu.CompilerParams(
            collective_id=0, has_side_effects=True, vmem_limit_bytes=56 * 2**20
        ),
        cost_estimate=pl.CostEstimate(flops=4 * 10**9, bytes_accessed=10**7, transcendentals=0),
    )(
        tokens, cotangent, weight_codes, weight_scales.T,
        weight_bits.reshape(1, 256), grad_bits.reshape(1, 256), table,
    )
    return pl.pallas_call(
        place, out_shape=shapes, in_specs=[vmem, vmem], out_specs=(vmem, vmem)
    )(*raw)


def solution(mesh):
    return jax.shard_map(
        on_device,
        mesh=mesh,
        in_specs=(
            P(("outer", "node"), None),
            P(("outer", "node"), None),
            P("node", None),
            P("node", None),
            P(),
            P(),
        ),
        out_specs=(P(("outer", "node"), None), P(("outer", "node"), None)),
        check_vma=False,
    )
```

```python
import math

import jax
import jax.numpy as jnp
import numpy as np
from jax import lax
from jax.experimental import pallas as pl
from jax.experimental.pallas import tpu as pltpu
from jax.sharding import PartitionSpec as P

MESH = pl.DeviceIdType.MESH
SHARD = 928
BLOCK = 58
WIN = 1024
EDGE = 96
HALF = SHARD // 2
END = 128
RUN = HALF - END
ROOT = 1.0 / math.sqrt(128.0)


def sylvester():
    row_index = np.arange(128).reshape(128, 1)
    column_index = np.arange(128).reshape(1, 128)
    parity = np.zeros((128, 128))
    for level in range(7):
        parity = parity + row_index // 2**level % 2 * (column_index // 2**level % 2)
    return 1.0 - 2.0 * (parity % 2)


def kernel(
    tokens, cot_in, codes, scales, wbits, gbits, table,
    out, grad,
    raw, tok, cot, wts, part, s1, d1, r1, s2, d2, r2, s3, d3, total, other, out_buf, grad_buf,
    tok_loc, tok_ss, tok_rs, cot_sem, code_sem, w_ss, w_rs, e_ss, e_rs, ss1, rs1, ss2, rs2, ss3, rs3, o_sem,
):
    o = lax.axis_index("outer")
    n = lax.axis_index("node")
    c = lax.rem(o, 2)
    x = lax.rem(o // 2, 4)
    ylo = o // 8
    yhi = n // 8
    z = lax.rem(n, 8)
    y = yhi * 2 + ylo
    odd = lax.rem(z + c, 2)

    def dev(cc, xx, yy, zz):
        xx, yy, zz = lax.rem(xx + 4, 4), lax.rem(yy + 4, 4), lax.rem(zz + 8, 8)
        return (lax.rem(yy, 2) * 8 + xx * 2 + cc, (yy // 2) * 8 + zz)

    mate = dev(1 - c, x, y, z)
    xp, xm = dev(c, x + 1, y, z), dev(c, x - 1, y, z)
    yp, ym = dev(c, x, y + 1, z), dev(c, x, y - 1, z)
    zp, zm = dev(c, x, y, z + 1), dev(c, x, y, z - 1)
    ypart = dev(c, x, 3 - y, z)
    xodd = lax.rem(x, 2)
    xpair, ypair = dev(c, x + 1 - 2 * xodd, y, z), dev(c, x, y + 1 - 2 * ylo, z)

    zero = jnp.zeros((EDGE, 256), jnp.bfloat16)

    @pl.loop(0, 8)
    def _(i):
        wts[i, pl.ds(0, EDGE)] = zero
        wts[i, pl.ds(WIN - EDGE, EDGE)] = zero

    barrier = pltpu.get_barrier_semaphore()
    peers = [mate, xp, xm, yp, ym] + [dev(c, x, y, z + k) for k in range(1, 8)]
    for p in peers:
        pl.semaphore_signal(barrier, inc=1, device_id=p, device_id_type=MESH)

    def start_of(g):
        return pl.multiple_of(g * SHARD - 32 * lax.rem(g, 4), 128)

    def order(i):
        if isinstance(i, int):
            i = jnp.int32(i)
        first = lax.rem(ylo + i, 2) * 4 + lax.rem(x + 2, 4)
        second = ylo * 4 + lax.rem(x + 1 + i, 4)
        third = (1 - ylo) * 4 + lax.rem(x + 2 + i, 4)
        return jnp.where(i < 2, first, jnp.where(i < 5, second, third))

    def local_tok(gi):
        return pltpu.make_async_copy(
            tokens.at[:, pl.ds(start_of(2 * gi + c), WIN)],
            tok.at[gi, pl.ds(pl.multiple_of(c * 256, 256), 256)],
            tok_loc.at[gi],
        )

    def swap_tok(gi):
        return pltpu.make_async_remote_copy(
            src_ref=tokens.at[:, pl.ds(start_of(2 * gi + 1 - c), WIN)],
            dst_ref=tok.at[gi, pl.ds(pl.multiple_of(c * 256, 256), 256)],
            send_sem=tok_ss.at[gi],
            recv_sem=tok_rs.at[gi],
            device_id=mate,
            device_id_type=MESH,
        )

    cot_mine = cot.at[pl.ds(pl.multiple_of(c * 256, 256), 256)]
    local_cot = pltpu.make_async_copy(cot_in, cot_mine, cot_sem.at[0])
    swap_cot = pltpu.make_async_remote_copy(
        src_ref=cot_in, dst_ref=cot_mine, send_sem=cot_sem.at[1], recv_sem=cot_sem.at[2],
        device_id=mate, device_id_type=MESH,
    )
    def local_codes(i):
        rows = pl.ds(i * HALF, HALF)
        return pltpu.make_async_copy(codes.at[rows], raw.at[rows], code_sem.at[i])

    @pl.when(odd == 0)
    def _():
        local_codes(0).start()
        local_codes(1).start()

    local_cot.start()

    @pl.loop(0, 8)
    def _(i):
        local_tok(order(i)).start()

    for h in range(2):
        for i in range(4):
            r1[h, i, pl.ds(HALF, 8)] = jnp.zeros((8, 128), jnp.float32)
    total[...] = jnp.zeros_like(total)

    def shard(yy, zz):
        zz = lax.rem(zz + 8, 8)
        slot = yy * 4 + zz // 2
        return slot, 32 * lax.rem(zz, 4)

    def rows_of(yy, zz, first, size):
        slot, base = shard(yy, zz)
        return wts.at[slot, pl.ds(pl.multiple_of(base + first, 16), size)]

    def move(ref, to, ss, rs):
        return pltpu.make_async_remote_copy(
            src_ref=ref, dst_ref=ref, send_sem=ss, recv_sem=rs, device_id=to, device_id_type=MESH
        )

    def push(yy, zz, to, k, i):
        slot, _ = shard(yy, zz)
        skip = (ylo, xodd)[i] * END
        return move(rows_of(yy, zz, i * HALF + skip, RUN), to, w_ss.at[k, i], w_rs.at[slot, i])

    def partner(yy, i):
        slot, _ = shard(yy, z)
        return move(rows_of(yy, z, i * HALF, HALF), ypart, w_ss.at[8, i], w_rs.at[slot, i])

    def swap_end(yy, zz, k, i):
        slot, _ = shard(yy, zz)
        own = (ylo, xodd)[i] * RUN
        return move(rows_of(yy, zz, i * HALF + own, END), (ypair, xpair)[i], e_ss.at[k, i], e_rs.at[slot, i])

    def passing(yy, zz, i, to=None, j=0):
        push(yy, zz, zp, 0, i).wait_recv()
        if to is not None:
            push(yy, zz, to, j, i).start()

    def complete(yy, zz):
        for i in range(2):
            swap_end(yy, zz, 0, i).wait_recv()

    near, far = yhi, 1 - yhi

    def multiply(j, side):
        dz0 = jnp.where(j < 2, 0, jnp.where(j < 6, jnp.where(lax.rem(j, 2) == 0, -2, 2), 4))
        far0 = jnp.where((j == 1) | (j == 4) | (j == 5) | (j == 7), 1, 0)
        dz1 = jnp.where(j < 4, 1, 3) * jnp.where(lax.rem(j, 2) == 0, -1, 1)
        far1 = jnp.where(lax.rem(j, 4) < 2, 0, 1)
        dz = jnp.where(odd == 0, dz0, dz1)
        off = jnp.where(odd == 0, far0, far1)
        slot = lax.rem(yhi + off, 2) * 4 + lax.rem(z + dz + 8, 8) // 2
        rows = pl.ds(pl.multiple_of(lax.rem(c + side, 2) * 256, 256), 256)
        total[side] += jnp.dot(tok[slot, rows], wts[slot], preferred_element_type=jnp.float32)

    def rotate_half(i):
        signs = (2 * wbits[...] - 1).astype(jnp.bfloat16)
        factors = (scales[...] * ROOT).T
        local_codes(i).wait()
        slot, base = shard(near, z)
        lo = i * HALF
        for b in range(2):
            cols = pl.ds(b * 128, 128)
            spun = jnp.dot(
                raw[pl.ds(lo, HALF), cols] * signs[:, b * 128:b * 128 + 128], table[...],
                preferred_element_type=jnp.float32,
            )
            spun = spun * factors[lo:lo + HALF, b:b + 1]
            wts[slot, pl.ds(pl.multiple_of(base + lo, 16), HALF), cols] = spun.astype(jnp.bfloat16)

    @pl.when(odd == 0)
    def _():
        rotate_half(0)

    pl.semaphore_wait(barrier, len(peers))

    swap_cot.start()

    def push_own(i):
        push(near, z, zp, 0, i).start()
        push(near, z, zm, 1, i).start()
        partner(near, i).start()

    @pl.when(odd == 0)
    def _():
        push_own(0)

    @pl.loop(0, 2)
    def _(i):
        swap_tok(order(i)).start()

    @pl.when(odd == 0)
    def _():
        rotate_half(1)
        push_own(1)

    @pl.loop(2, 8)
    def _(i):
        swap_tok(order(i)).start()

    local_cot.wait()
    swap_cot.wait_recv()

    def produce(i):
        gi = order(i)
        local_tok(gi).wait()
        swap_tok(gi).wait_recv()
        sums = lax.dot_general(
            tok[gi], cot[...], (((0,), (0,)), ((), ())), preferred_element_type=jnp.float32
        )
        part[0, gi] = sums[:, :128]
        part[1, gi] = sums[:, 128:]

    def ring(level, h):
        along_x = (h == 0) == (level == 1)
        pos = x if along_x else y
        ends = (xp, xm) if along_x else (yp, ym)
        sent, got = (s1, d1) if level == 1 else (s2, d2)
        ssem, rsem = (ss1, rs1) if level == 1 else (ss2, rs2)
        total = r1 if level == 1 else r2

        def copy(way, m, piece=None):
            place_of = (h, way, m) if piece is None else (h, way, 2, piece)
            return pltpu.make_async_remote_copy(
                src_ref=sent.at[place_of], dst_ref=got.at[place_of],
                send_sem=ssem.at[h, way, m], recv_sem=rsem.at[h, way, m],
                device_id=ends[way], device_id_type=MESH,
            )

        count = 2 if level == 1 else 4
        first = 1 - yhi if h == 0 else 0
        turn = (first, 1 - first)

        def read(dest, half, i):
            if level == 1:
                gi = half * 4 + dest if h == 0 else lax.rem(dest, 2) * 4 + lax.rem(x + 2 + 2 * half + i, 4)
                top = 32 * lax.rem(2 * gi + c, 4) + (i if h == 0 else dest // 2) * HALF
                return part[h, gi, pl.ds(pl.multiple_of(top, 16), HALF)]
            block = lax.rem(dest, 2) * 2 + dest // 2 if h == 0 else lax.rem(dest - x + 6, 4)
            return r1[h, block, pl.ds(BLOCK * (half * 4 + i), 64)]

        def send(way, m):
            off = (2, 1, 1)[m] if way == 0 else (2, 3, 3)[m]
            dest = lax.rem(pos + off, 4)
            half = (0, 1, 0)[m] if way == 0 else (1, 0, 1)[m]
            if m == 2:
                copy(way, 0).wait_recv()
            for j in range(count):
                i = turn[j] if level == 1 and m == 2 else j
                value = read(dest, half, i)
                if m == 2:
                    value = value + got[h, way, 0, i].astype(jnp.float32)
                sent[h, way, m, i] = value.astype(jnp.bfloat16)
                if level == 1 and m == 2:
                    copy(way, 2 + j, i).start()
            if level == 2 or m < 2:
                copy(way, m).start()

        def finish(j=0):
            for half in range(2):
                a, b = ((0, 2), (1, 1)) if half == 0 else ((0, 1), (1, 2))
                for way, m in (b, a):
                    if level == 1 and m == 2:
                        copy(way, 2 + j, turn[j]).wait_recv()
                    elif j == 0:
                        copy(way, m).wait_recv()
                for i in ((turn[j],) if level == 1 else range(count)):
                    value = (
                        read(pos, half, i)
                        + got[(h,) + a + (i,)].astype(jnp.float32)
                        + got[(h,) + b + (i,)].astype(jnp.float32)
                    )
                    if level == 1:
                        r1[h, half * 2 + i, pl.ds(0, HALF)] = value
                    else:
                        r2[half * 4 + i, h] = value

        def drain():
            for way in range(2):
                for m in range(4 if level == 1 else 3):
                    copy(way, m, turn[m - 2] if level == 1 and m > 1 else None).wait_send()

        return send, finish, drain

    send_a, finish_a, drain_a = ring(1, 0)
    send_b, finish_b, drain_b = ring(1, 1)
    send_c, finish_c, drain_c = ring(2, 0)
    send_d, finish_d, drain_d = ring(2, 1)

    def last(h, k):
        to = lax.rem(z + k, 8)
        return pltpu.make_async_remote_copy(
            src_ref=s3.at[h, to], dst_ref=d3.at[h, k - 1],
            send_sem=ss3.at[h, k - 1], recv_sem=rs3.at[h, k - 1],
            device_id=dev(c, x, y, z + k), device_id_type=MESH,
        )

    def last_sends(h):
        for i in range(8):
            s3[h, i] = r2[i, h].astype(jnp.bfloat16)
        for k in (4, 3, 5, 2, 6, 1, 7):
            last(h, k).start()

    def far_own(i):
        partner(far, i).wait_recv()
        push(far, z, zp, 2, i).start()
        push(far, z, zm, 3, i).start()

    def pass_pair(yy, d, i, first, second):
        passing(yy, z - d, i, *first)
        passing(yy, z + d, i, *second)

    def ends(yy, d, k, i):
        swap_end(yy, z - d, k, i).start()
        swap_end(yy, z + d, k + 1, i).start()

    def both(yy, d):
        complete(yy, z - d)
        complete(yy, z + d)

    def ring_start(send, *ms):
        for m in ms:
            send(0, m)
            send(1, m)

    def product(first, last_one, *sides):
        for side in sides:
            pl.loop(first, last_one)(lambda j: multiply(j, side))

    def run(who, act):
        if who == 2:
            act()
        else:
            pl.when(odd == who)(act)

    swap_out = pltpu.make_async_remote_copy(
        src_ref=total.at[1], dst_ref=other, send_sem=o_sem.at[0], recv_sem=o_sem.at[1],
        device_id=mate, device_id_type=MESH,
    )
    write_out = pltpu.make_async_copy(out_buf, out, o_sem.at[2])
    write_grad = pltpu.make_async_copy(grad_buf, grad, o_sem.at[3])

    steps = [
        (2.5, 2, lambda: pl.loop(0, 2)(produce)),
        (2.6, 2, lambda: ring_start(send_a, 0)),
        (3.3, 1, lambda: pass_pair(near, 1, 0, (zp, 0), (zm, 1))),
        (3.33, 1, lambda: ends(near, 1, 0, 0)),
        (4.5, 2, lambda: pl.loop(2, 3)(produce)),
        (5.4, 1, lambda: pass_pair(near, 1, 1, (zp, 0), (zm, 1))),
        (5.43, 1, lambda: ends(near, 1, 0, 1)),
        (5.98, 2, lambda: send_b(0, 0)),
        (6.0, 2, lambda: pl.loop(3, 5)(produce)),
        (6.1, 2, lambda: send_b(1, 0)),
        (6.78, 0, lambda: far_own(0)),
        (7.0, 1, lambda: pass_pair(far, 1, 0, (zp, 2), (zm, 3))),
        (7.03, 1, lambda: ends(far, 1, 2, 0)),
        (8.78, 0, lambda: far_own(1)),
        (9.0, 2, lambda: pl.loop(5, 8)(produce)),
        (9.01, 1, lambda: pass_pair(far, 1, 1, (zp, 2), (zm, 3))),
        (9.03, 1, lambda: ends(far, 1, 2, 1)),
        (9.1, 2, lambda: ring_start(send_a, 1)),
        (9.2, 2, lambda: ring_start(send_b, 1)),
        (10.5, 2, lambda: ring_start(send_a, 2)),
        (10.78, 0, lambda: pass_pair(near, 2, 0, (zp, 4), (zm, 5))),
        (10.8, 0, lambda: ends(near, 2, 0, 0)),
        (12.78, 0, lambda: pass_pair(near, 2, 1, (zp, 4), (zm, 5))),
        (12.8, 0, lambda: ends(near, 2, 0, 1)),
        (13.5, 2, lambda: ring_start(send_b, 2)),
        (14.1, 1, lambda: pass_pair(near, 3, 0, (zp, 4), ())),
        (14.13, 1, lambda: ends(near, 3, 4, 0)),
        (14.88, 0, lambda: pass_pair(far, 2, 0, (zp, 6), (zm, 7))),
        (14.9, 0, lambda: ends(far, 2, 2, 0)),
        (15.7, 1, lambda: both(far, 1)),
        (16.0, 1, lambda: pass_pair(near, 3, 1, (zp, 4), ())),
        (16.03, 1, lambda: ends(near, 3, 4, 1)),
        (16.78, 0, lambda: pass_pair(far, 2, 1, (zp, 6), (zm, 7))),
        (16.8, 0, lambda: ends(far, 2, 2, 1)),
        (16.81, 1, lambda: both(near, 1)),
        (16.9, 0, lambda: both(near, 2)),
        (17.0, 2, lambda: product(0, 4, 1, 0)),
        (19.5, 2, finish_a),
        (19.6, 2, lambda: ring_start(send_c, 0)),
        (20.5, 2, lambda: finish_a(1)),
        (20.6, 2, lambda: ring_start(send_c, 1)),
        (21.5, 2, finish_b),
        (21.6, 2, lambda: ring_start(send_d, 0)),
        (21.78, 0, lambda: passing(near, z + 4, 0)),
        (21.8, 0, lambda: swap_end(near, z + 4, 4, 0).start()),
        (21.9, 1, lambda: pass_pair(far, 3, 1, (), (zm, 5))),
        (21.93, 1, lambda: ends(far, 3, 6, 1)),
        (22.02, 1, lambda: pass_pair(far, 3, 0, (), (zm, 5))),
        (22.04, 1, lambda: ends(far, 3, 6, 0)),
        (22.4, 2, lambda: ring_start(send_c, 2)),
        (23.0, 2, lambda: finish_b(1)),
        (23.1, 2, lambda: ring_start(send_d, 1)),
        (24.28, 0, lambda: passing(near, z + 4, 1)),
        (24.3, 0, lambda: swap_end(near, z + 4, 4, 1).start()),
        (24.5, 2, lambda: ring_start(send_d, 2)),
        (24.9, 0, lambda: both(far, 2)),
        (24.91, 1, lambda: both(near, 3)),
        (25.0, 2, lambda: product(4, 6, 1, 0)),
        (25.5, 2, finish_c),
        (25.52, 2, lambda: last_sends(0)),
        (28.2, 0, lambda: passing(far, z + 4, 0)),
        (28.22, 0, lambda: swap_end(far, z + 4, 5, 0).start()),
        (28.5, 2, finish_d),
        (28.6, 2, lambda: last_sends(1)),
        (30.66, 0, lambda: passing(far, z + 4, 1)),
        (30.68, 0, lambda: swap_end(far, z + 4, 5, 1).start()),
        (35.8, 0, lambda: complete(near, z + 4)),
        (35.9, 0, lambda: complete(far, z + 4)),
        (35.91, 1, lambda: both(far, 3)),
        (36.0, 2, lambda: product(6, 8, 1)),
        (36.1, 2, lambda: swap_out.start()),
        (38.95, 2, lambda: product(6, 8, 0)),
    ]
    for _, who, act in sorted(steps, key=lambda step: step[0]):
        run(who, act)

    gsigns = (2 * gbits[...] - 1).astype(jnp.float32)
    for h in range(2):
        value = r2[z, h]
        for k in range(1, 8):
            last(h, k).wait_recv()
            value = value + d3[h, k - 1].astype(jnp.float32)
        value = value * gsigns[:, h * 128:h * 128 + 128]
        spun = jnp.zeros((64, 128), jnp.float32)
        for _ in range(3):
            head = value.astype(jnp.bfloat16)
            spun = spun + jnp.dot(head, table[...], preferred_element_type=jnp.float32)
            value = value - head.astype(jnp.float32)
        grad_buf[:, h * 128:h * 128 + 128] = (spun * ROOT)[:BLOCK]
    write_grad.start()

    swap_out.wait_recv()
    out_buf[...] = (total[0] + other[...]).astype(jnp.bfloat16)
    write_out.start()

    swap_out.wait_send()
    swap_cot.wait_send()

    @pl.loop(0, 8)
    def _(i):
        swap_tok(i).wait_send()

    drain_a()
    drain_b()
    drain_c()
    drain_d()
    for h in range(2):
        for k in range(1, 8):
            last(h, k).wait_send()

    def sent_all(pushes, ends):
        for i in range(2):
            for k in range(pushes):
                push(near, z + odd, zp, k, i).wait_send()
            for k in range(ends):
                swap_end(near, z + odd, k, i).wait_send()

    def sent_even():
        for i in range(2):
            partner(near, i).wait_send()
        sent_all(8, 6)

    run(0, sent_even)
    run(1, lambda: sent_all(6, 8))
    write_grad.wait()
    write_out.wait()


def place(out_in, grad_in, out, grad):
    out[...] = out_in[...]
    grad[...] = grad_in[...]


def on_device(tokens, cotangent, weight_codes, weight_scales, weight_bits, grad_bits):
    table = jnp.asarray(sylvester(), jnp.bfloat16)
    vmem = pl.BlockSpec(memory_space=pltpu.VMEM)
    hbm = pl.BlockSpec(memory_space=pl.ANY)
    dma = pltpu.SemaphoreType.DMA
    bf, f32 = jnp.bfloat16, jnp.float32
    shapes = (jax.ShapeDtypeStruct((256, 256), bf), jax.ShapeDtypeStruct((BLOCK, 256), f32))
    raw = pl.pallas_call(
        kernel,
        out_shape=shapes,
        in_specs=[hbm, hbm, hbm, vmem, vmem, vmem, vmem],
        out_specs=(hbm, hbm),
        scratch_shapes=[
            pltpu.VMEM((SHARD, 256), bf),
            pltpu.VMEM((8, 512, WIN), bf),
            pltpu.VMEM((512, 256), bf),
            pltpu.VMEM((8, WIN, 256), bf),
            pltpu.VMEM((2, 8, WIN, 128), f32),
            pltpu.VMEM((2, 2, 3, 2, HALF, 128), bf),
            pltpu.VMEM((2, 2, 3, 2, HALF, 128), bf),
            pltpu.VMEM((2, 4, HALF + 8, 128), f32),
            pltpu.VMEM((2, 2, 3, 4, 64, 128), bf),
            pltpu.VMEM((2, 2, 3, 4, 64, 128), bf),
            pltpu.VMEM((8, 2, 64, 128), f32),
            pltpu.VMEM((2, 8, 64, 128), bf),
            pltpu.VMEM((2, 7, 64, 128), bf),
            pltpu.VMEM((2, 256, 256), f32),
            pltpu.VMEM((256, 256), f32),
            pltpu.VMEM((256, 256), bf),
            pltpu.VMEM((BLOCK, 256), f32),
            dma((8,)), dma((8,)), dma((8,)), dma((3,)), dma((2,)),
            dma((9, 2)), dma((8, 2)), dma((8, 2)), dma((8, 2)),
            dma((2, 2, 4)), dma((2, 2, 4)), dma((2, 2, 3)), dma((2, 2, 3)),
            dma((2, 7)), dma((2, 7)), dma((4,)),
        ],
        compiler_params=pltpu.CompilerParams(
            collective_id=0, has_side_effects=True, vmem_limit_bytes=56 * 2**20
        ),
        cost_estimate=pl.CostEstimate(flops=4 * 10**9, bytes_accessed=10**7, transcendentals=0),
    )(
        tokens, cotangent, weight_codes, weight_scales.T,
        weight_bits.reshape(1, 256), grad_bits.reshape(1, 256), table,
    )
    return pl.pallas_call(
        place, out_shape=shapes, in_specs=[vmem, vmem], out_specs=(vmem, vmem)
    )(*raw)


def solution(mesh):
    return jax.shard_map(
        on_device,
        mesh=mesh,
        in_specs=(
            P(("outer", "node"), None),
            P(("outer", "node"), None),
            P("node", None),
            P("node", None),
            P(),
            P(),
        ),
        out_specs=(P(("outer", "node"), None), P(("outer", "node"), None)),
        check_vma=False,
    )
```

```python
import math

import jax
import jax.numpy as jnp
import numpy as np
from jax import lax
from jax.experimental import pallas as pl
from jax.experimental.pallas import tpu as pltpu
from jax.sharding import PartitionSpec as P

MESH = pl.DeviceIdType.MESH
SHARD = 928
BLOCK = 58
WIN = 1024
EDGE = 96
HALF = SHARD // 2
END = 128
RUN = HALF - END
ROOT = 1.0 / math.sqrt(128.0)


def sylvester():
    row_index = np.arange(128).reshape(128, 1)
    column_index = np.arange(128).reshape(1, 128)
    parity = np.zeros((128, 128))
    for level in range(7):
        parity = parity + row_index // 2**level % 2 * (column_index // 2**level % 2)
    return 1.0 - 2.0 * (parity % 2)


def kernel(
    tokens, cot_in, codes, scales_in, wbits_in, gbits_in, table_in,
    out, grad,
    scales, wbits, gbits, table, raw, tok, cot, wts, part, s1, d1, r1, s2, d2, r2, s3, d3, total, other, out_buf, grad_buf,
    tok_loc, tok_ss, tok_rs, cot_sem, code_sem, small_sem, w_ss, w_rs, e_ss, e_rs, ss1, rs1, ss2, rs2, ss3, rs3, o_sem,
):
    o = lax.axis_index("outer")
    n = lax.axis_index("node")
    c = lax.rem(o, 2)
    x = lax.rem(o // 2, 4)
    ylo = o // 8
    yhi = n // 8
    z = lax.rem(n, 8)
    y = yhi * 2 + ylo
    odd = lax.rem(z + c, 2)

    def dev(cc, xx, yy, zz):
        xx, yy, zz = lax.rem(xx + 4, 4), lax.rem(yy + 4, 4), lax.rem(zz + 8, 8)
        return (lax.rem(yy, 2) * 8 + xx * 2 + cc, (yy // 2) * 8 + zz)

    mate = dev(1 - c, x, y, z)
    xp, xm = dev(c, x + 1, y, z), dev(c, x - 1, y, z)
    yp, ym = dev(c, x, y + 1, z), dev(c, x, y - 1, z)
    zp, zm = dev(c, x, y, z + 1), dev(c, x, y, z - 1)
    ypart = dev(c, x, 3 - y, z)
    xodd = lax.rem(x, 2)
    xpair, ypair = dev(c, x + 1 - 2 * xodd, y, z), dev(c, x, y + 1 - 2 * ylo, z)

    small = [
        pltpu.make_async_copy(source, target, small_sem.at[i])
        for i, (source, target) in enumerate(
            ((scales_in, scales), (wbits_in, wbits), (gbits_in, gbits), (table_in, table))
        )
    ]

    zero = jnp.zeros((EDGE, 256), jnp.bfloat16)

    @pl.loop(0, 8)
    def _(i):
        wts[i, pl.ds(0, EDGE)] = zero
        wts[i, pl.ds(WIN - EDGE, EDGE)] = zero

    barrier = pltpu.get_barrier_semaphore()
    peers = [mate, xp, xm, yp, ym] + [dev(c, x, y, z + k) for k in range(1, 8)]
    for p in peers:
        pl.semaphore_signal(barrier, inc=1, device_id=p, device_id_type=MESH)

    for copy_in in small:
        copy_in.start()

    def start_of(g):
        return pl.multiple_of(g * SHARD - 32 * lax.rem(g, 4), 128)

    def order(i):
        if isinstance(i, int):
            i = jnp.int32(i)
        first = lax.rem(ylo + i, 2) * 4 + lax.rem(x + 2, 4)
        second = ylo * 4 + lax.rem(x + 1 + i, 4)
        third = (1 - ylo) * 4 + lax.rem(x + 2 + i, 4)
        return jnp.where(i < 2, first, jnp.where(i < 5, second, third))

    def local_tok(gi):
        return pltpu.make_async_copy(
            tokens.at[:, pl.ds(start_of(2 * gi + c), WIN)],
            tok.at[gi, pl.ds(pl.multiple_of(c * 256, 256), 256)],
            tok_loc.at[gi],
        )

    def swap_tok(gi):
        return pltpu.make_async_remote_copy(
            src_ref=tokens.at[:, pl.ds(start_of(2 * gi + 1 - c), WIN)],
            dst_ref=tok.at[gi, pl.ds(pl.multiple_of(c * 256, 256), 256)],
            send_sem=tok_ss.at[gi],
            recv_sem=tok_rs.at[gi],
            device_id=mate,
            device_id_type=MESH,
        )

    cot_mine = cot.at[pl.ds(pl.multiple_of(c * 256, 256), 256)]
    local_cot = pltpu.make_async_copy(cot_in, cot_mine, cot_sem.at[0])
    swap_cot = pltpu.make_async_remote_copy(
        src_ref=cot_in, dst_ref=cot_mine, send_sem=cot_sem.at[1], recv_sem=cot_sem.at[2],
        device_id=mate, device_id_type=MESH,
    )
    def local_codes(i):
        rows = pl.ds(i * HALF, HALF)
        return pltpu.make_async_copy(codes.at[rows], raw.at[rows], code_sem.at[i])

    @pl.when(odd == 0)
    def _():
        local_codes(0).start()
        local_codes(1).start()

    local_cot.start()

    @pl.loop(0, 8)
    def _(i):
        local_tok(order(i)).start()

    for h in range(2):
        for i in range(4):
            r1[h, i, pl.ds(HALF, 8)] = jnp.zeros((8, 128), jnp.float32)
    total[...] = jnp.zeros_like(total)

    def shard(yy, zz):
        zz = lax.rem(zz + 8, 8)
        slot = yy * 4 + zz // 2
        return slot, 32 * lax.rem(zz, 4)

    def rows_of(yy, zz, first, size):
        slot, base = shard(yy, zz)
        return wts.at[slot, pl.ds(pl.multiple_of(base + first, 16), size)]

    def move(ref, to, ss, rs):
        return pltpu.make_async_remote_copy(
            src_ref=ref, dst_ref=ref, send_sem=ss, recv_sem=rs, device_id=to, device_id_type=MESH
        )

    def push(yy, zz, to, k, i):
        slot, _ = shard(yy, zz)
        skip = (ylo, xodd)[i] * END
        return move(rows_of(yy, zz, i * HALF + skip, RUN), to, w_ss.at[k, i], w_rs.at[slot, i])

    def partner(yy, i):
        slot, _ = shard(yy, z)
        return move(rows_of(yy, z, i * HALF, HALF), ypart, w_ss.at[8, i], w_rs.at[slot, i])

    def swap_end(yy, zz, k, i):
        slot, _ = shard(yy, zz)
        own = (ylo, xodd)[i] * RUN
        return move(rows_of(yy, zz, i * HALF + own, END), (ypair, xpair)[i], e_ss.at[k, i], e_rs.at[slot, i])

    def passing(yy, zz, i, to=None, j=0):
        push(yy, zz, zp, 0, i).wait_recv()
        if to is not None:
            push(yy, zz, to, j, i).start()

    def complete(yy, zz):
        for i in range(2):
            swap_end(yy, zz, 0, i).wait_recv()

    near, far = yhi, 1 - yhi

    def multiply(j, side):
        dz0 = jnp.where(j < 2, 0, jnp.where(j < 6, jnp.where(lax.rem(j, 2) == 0, -2, 2), 4))
        far0 = jnp.where((j == 1) | (j == 4) | (j == 5) | (j == 7), 1, 0)
        dz1 = jnp.where(j < 4, 1, 3) * jnp.where(lax.rem(j, 2) == 0, -1, 1)
        far1 = jnp.where(lax.rem(j, 4) < 2, 0, 1)
        dz = jnp.where(odd == 0, dz0, dz1)
        off = jnp.where(odd == 0, far0, far1)
        slot = lax.rem(yhi + off, 2) * 4 + lax.rem(z + dz + 8, 8) // 2
        rows = pl.ds(pl.multiple_of(lax.rem(c + side, 2) * 256, 256), 256)
        total[side] += jnp.dot(tok[slot, rows], wts[slot], preferred_element_type=jnp.float32)

    def rotate_half(i):
        signs = (2 * wbits[...] - 1).astype(jnp.bfloat16)
        factors = (scales[...] * ROOT).T
        local_codes(i).wait()
        slot, base = shard(near, z)
        lo = i * HALF
        for b in range(2):
            cols = pl.ds(b * 128, 128)
            spun = jnp.dot(
                raw[pl.ds(lo, HALF), cols] * signs[:, b * 128:b * 128 + 128], table[...],
                preferred_element_type=jnp.float32,
            )
            spun = spun * factors[lo:lo + HALF, b:b + 1]
            wts[slot, pl.ds(pl.multiple_of(base + lo, 16), HALF), cols] = spun.astype(jnp.bfloat16)

    for copy_in in small:
        copy_in.wait()

    @pl.when(odd == 0)
    def _():
        rotate_half(0)

    pl.semaphore_wait(barrier, len(peers))

    swap_cot.start()

    def push_own(i):
        push(near, z, zp, 0, i).start()
        push(near, z, zm, 1, i).start()
        partner(near, i).start()

    @pl.when(odd == 0)
    def _():
        push_own(0)

    @pl.loop(0, 2)
    def _(i):
        swap_tok(order(i)).start()

    @pl.when(odd == 0)
    def _():
        rotate_half(1)
        push_own(1)

    @pl.loop(2, 8)
    def _(i):
        swap_tok(order(i)).start()

    local_cot.wait()
    swap_cot.wait_recv()

    def produce(i):
        gi = order(i)
        local_tok(gi).wait()
        swap_tok(gi).wait_recv()
        sums = lax.dot_general(
            tok[gi], cot[...], (((0,), (0,)), ((), ())), preferred_element_type=jnp.float32
        )
        part[0, gi] = sums[:, :128]
        part[1, gi] = sums[:, 128:]

    def ring(level, h):
        along_x = (h == 0) == (level == 1)
        pos = x if along_x else y
        ends = (xp, xm) if along_x else (yp, ym)
        sent, got = (s1, d1) if level == 1 else (s2, d2)
        ssem, rsem = (ss1, rs1) if level == 1 else (ss2, rs2)
        total = r1 if level == 1 else r2

        def copy(way, m, piece=None):
            place_of = (h, way, m) if piece is None else (h, way, 2, piece)
            return pltpu.make_async_remote_copy(
                src_ref=sent.at[place_of], dst_ref=got.at[place_of],
                send_sem=ssem.at[h, way, m], recv_sem=rsem.at[h, way, m],
                device_id=ends[way], device_id_type=MESH,
            )

        count = 2 if level == 1 else 4
        first = 1 - yhi if h == 0 else 0
        turn = (first, 1 - first)

        def read(dest, half, i):
            if level == 1:
                gi = half * 4 + dest if h == 0 else lax.rem(dest, 2) * 4 + lax.rem(x + 2 + 2 * half + i, 4)
                top = 32 * lax.rem(2 * gi + c, 4) + (i if h == 0 else dest // 2) * HALF
                return part[h, gi, pl.ds(pl.multiple_of(top, 16), HALF)]
            block = lax.rem(dest, 2) * 2 + dest // 2 if h == 0 else lax.rem(dest - x + 6, 4)
            return r1[h, block, pl.ds(BLOCK * (half * 4 + i), 64)]

        def send(way, m):
            off = (2, 1, 1)[m] if way == 0 else (2, 3, 3)[m]
            dest = lax.rem(pos + off, 4)
            half = (0, 1, 0)[m] if way == 0 else (1, 0, 1)[m]
            if m == 2:
                copy(way, 0).wait_recv()
            for j in range(count):
                i = turn[j] if level == 1 and m == 2 else j
                value = read(dest, half, i)
                if m == 2:
                    value = value + got[h, way, 0, i].astype(jnp.float32)
                sent[h, way, m, i] = value.astype(jnp.bfloat16)
                if level == 1 and m == 2:
                    copy(way, 2 + j, i).start()
            if level == 2 or m < 2:
                copy(way, m).start()

        def finish(j=0):
            for half in range(2):
                a, b = ((0, 2), (1, 1)) if half == 0 else ((0, 1), (1, 2))
                for way, m in (b, a):
                    if level == 1 and m == 2:
                        copy(way, 2 + j, turn[j]).wait_recv()
                    elif j == 0:
                        copy(way, m).wait_recv()
                for i in ((turn[j],) if level == 1 else range(count)):
                    value = (
                        read(pos, half, i)
                        + got[(h,) + a + (i,)].astype(jnp.float32)
                        + got[(h,) + b + (i,)].astype(jnp.float32)
                    )
                    if level == 1:
                        r1[h, half * 2 + i, pl.ds(0, HALF)] = value
                    else:
                        r2[half * 4 + i, h] = value

        def drain():
            for way in range(2):
                for m in range(4 if level == 1 else 3):
                    copy(way, m, turn[m - 2] if level == 1 and m > 1 else None).wait_send()

        return send, finish, drain

    send_a, finish_a, drain_a = ring(1, 0)
    send_b, finish_b, drain_b = ring(1, 1)
    send_c, finish_c, drain_c = ring(2, 0)
    send_d, finish_d, drain_d = ring(2, 1)

    def last(h, k):
        to = lax.rem(z + k, 8)
        return pltpu.make_async_remote_copy(
            src_ref=s3.at[h, to], dst_ref=d3.at[h, k - 1],
            send_sem=ss3.at[h, k - 1], recv_sem=rs3.at[h, k - 1],
            device_id=dev(c, x, y, z + k), device_id_type=MESH,
        )

    def last_sends(h):
        for i in range(8):
            s3[h, i] = r2[i, h].astype(jnp.bfloat16)
        for k in (4, 3, 5, 2, 6, 1, 7):
            last(h, k).start()

    def far_own(i):
        partner(far, i).wait_recv()
        push(far, z, zp, 2, i).start()
        push(far, z, zm, 3, i).start()

    def pass_pair(yy, d, i, first, second):
        passing(yy, z - d, i, *first)
        passing(yy, z + d, i, *second)

    def ends(yy, d, k, i):
        swap_end(yy, z - d, k, i).start()
        swap_end(yy, z + d, k + 1, i).start()

    def both(yy, d):
        complete(yy, z - d)
        complete(yy, z + d)

    def ring_start(send, *ms):
        for m in ms:
            send(0, m)
            send(1, m)

    def product(first, last_one, *sides):
        for side in sides:
            pl.loop(first, last_one)(lambda j: multiply(j, side))

    def run(who, act):
        if who == 2:
            act()
        else:
            pl.when(odd == who)(act)

    swap_out = pltpu.make_async_remote_copy(
        src_ref=total.at[1], dst_ref=other, send_sem=o_sem.at[0], recv_sem=o_sem.at[1],
        device_id=mate, device_id_type=MESH,
    )
    write_out = pltpu.make_async_copy(out_buf, out, o_sem.at[2])
    write_grad = pltpu.make_async_copy(grad_buf, grad, o_sem.at[3])

    steps = [
        (2.5, 2, lambda: pl.loop(0, 2)(produce)),
        (2.6, 2, lambda: ring_start(send_a, 0)),
        (3.3, 1, lambda: pass_pair(near, 1, 0, (zp, 0), (zm, 1))),
        (3.33, 1, lambda: ends(near, 1, 0, 0)),
        (4.5, 2, lambda: pl.loop(2, 3)(produce)),
        (5.4, 1, lambda: pass_pair(near, 1, 1, (zp, 0), (zm, 1))),
        (5.43, 1, lambda: ends(near, 1, 0, 1)),
        (5.98, 2, lambda: send_b(0, 0)),
        (6.0, 2, lambda: pl.loop(3, 5)(produce)),
        (6.1, 2, lambda: send_b(1, 0)),
        (6.78, 0, lambda: far_own(0)),
        (7.0, 1, lambda: pass_pair(far, 1, 0, (zp, 2), (zm, 3))),
        (7.03, 1, lambda: ends(far, 1, 2, 0)),
        (8.78, 0, lambda: far_own(1)),
        (9.0, 2, lambda: pl.loop(5, 8)(produce)),
        (9.01, 1, lambda: pass_pair(far, 1, 1, (zp, 2), (zm, 3))),
        (9.03, 1, lambda: ends(far, 1, 2, 1)),
        (9.1, 2, lambda: ring_start(send_a, 1)),
        (9.2, 2, lambda: ring_start(send_b, 1)),
        (10.5, 2, lambda: ring_start(send_a, 2)),
        (10.78, 0, lambda: pass_pair(near, 2, 0, (zp, 4), (zm, 5))),
        (10.8, 0, lambda: ends(near, 2, 0, 0)),
        (12.78, 0, lambda: pass_pair(near, 2, 1, (zp, 4), (zm, 5))),
        (12.8, 0, lambda: ends(near, 2, 0, 1)),
        (13.5, 2, lambda: ring_start(send_b, 2)),
        (14.1, 1, lambda: pass_pair(near, 3, 0, (zp, 4), ())),
        (14.13, 1, lambda: ends(near, 3, 4, 0)),
        (14.88, 0, lambda: pass_pair(far, 2, 0, (zp, 6), (zm, 7))),
        (14.9, 0, lambda: ends(far, 2, 2, 0)),
        (15.7, 1, lambda: both(far, 1)),
        (16.0, 1, lambda: pass_pair(near, 3, 1, (zp, 4), ())),
        (16.03, 1, lambda: ends(near, 3, 4, 1)),
        (16.78, 0, lambda: pass_pair(far, 2, 1, (zp, 6), (zm, 7))),
        (16.8, 0, lambda: ends(far, 2, 2, 1)),
        (16.81, 1, lambda: both(near, 1)),
        (16.9, 0, lambda: both(near, 2)),
        (17.0, 2, lambda: product(0, 4, 1, 0)),
        (19.5, 2, finish_a),
        (19.6, 2, lambda: ring_start(send_c, 0)),
        (20.5, 2, lambda: finish_a(1)),
        (20.6, 2, lambda: ring_start(send_c, 1)),
        (21.5, 2, finish_b),
        (21.6, 2, lambda: ring_start(send_d, 0)),
        (21.78, 0, lambda: passing(near, z + 4, 0)),
        (21.8, 0, lambda: swap_end(near, z + 4, 4, 0).start()),
        (21.9, 1, lambda: pass_pair(far, 3, 1, (), (zm, 5))),
        (21.93, 1, lambda: ends(far, 3, 6, 1)),
        (22.02, 1, lambda: pass_pair(far, 3, 0, (), (zm, 5))),
        (22.04, 1, lambda: ends(far, 3, 6, 0)),
        (22.4, 2, lambda: ring_start(send_c, 2)),
        (23.0, 2, lambda: finish_b(1)),
        (23.1, 2, lambda: ring_start(send_d, 1)),
        (24.28, 0, lambda: passing(near, z + 4, 1)),
        (24.3, 0, lambda: swap_end(near, z + 4, 4, 1).start()),
        (24.5, 2, lambda: ring_start(send_d, 2)),
        (24.9, 0, lambda: both(far, 2)),
        (24.91, 1, lambda: both(near, 3)),
        (25.0, 2, lambda: product(4, 6, 1, 0)),
        (25.5, 2, finish_c),
        (25.52, 2, lambda: last_sends(0)),
        (28.2, 0, lambda: passing(far, z + 4, 0)),
        (28.22, 0, lambda: swap_end(far, z + 4, 5, 0).start()),
        (28.5, 2, finish_d),
        (28.6, 2, lambda: last_sends(1)),
        (30.66, 0, lambda: passing(far, z + 4, 1)),
        (30.68, 0, lambda: swap_end(far, z + 4, 5, 1).start()),
        (35.8, 0, lambda: complete(near, z + 4)),
        (35.9, 0, lambda: complete(far, z + 4)),
        (35.91, 1, lambda: both(far, 3)),
        (36.0, 2, lambda: product(6, 8, 1)),
        (36.1, 2, lambda: swap_out.start()),
        (38.95, 2, lambda: product(6, 8, 0)),
    ]
    for _, who, act in sorted(steps, key=lambda step: step[0]):
        run(who, act)

    gsigns = (2 * gbits[...] - 1).astype(jnp.float32)
    for h in range(2):
        value = r2[z, h]
        for k in range(1, 8):
            last(h, k).wait_recv()
            value = value + d3[h, k - 1].astype(jnp.float32)
        value = value * gsigns[:, h * 128:h * 128 + 128]
        spun = jnp.zeros((64, 128), jnp.float32)
        for _ in range(3):
            head = value.astype(jnp.bfloat16)
            spun = spun + jnp.dot(head, table[...], preferred_element_type=jnp.float32)
            value = value - head.astype(jnp.float32)
        grad_buf[:, h * 128:h * 128 + 128] = (spun * ROOT)[:BLOCK]
    write_grad.start()

    swap_out.wait_recv()
    out_buf[...] = (total[0] + other[...]).astype(jnp.bfloat16)
    write_out.start()

    swap_out.wait_send()
    swap_cot.wait_send()

    @pl.loop(0, 8)
    def _(i):
        swap_tok(i).wait_send()

    drain_a()
    drain_b()
    drain_c()
    drain_d()
    for h in range(2):
        for k in range(1, 8):
            last(h, k).wait_send()

    def sent_all(pushes, ends):
        for i in range(2):
            for k in range(pushes):
                push(near, z + odd, zp, k, i).wait_send()
            for k in range(ends):
                swap_end(near, z + odd, k, i).wait_send()

    def sent_even():
        for i in range(2):
            partner(near, i).wait_send()
        sent_all(8, 6)

    run(0, sent_even)
    run(1, lambda: sent_all(6, 8))
    write_grad.wait()
    write_out.wait()


def place(out_in, grad_in, out, grad):
    out[...] = out_in[...]
    grad[...] = grad_in[...]


def on_device(tokens, cotangent, weight_codes, weight_scales, weight_bits, grad_bits):
    table = jnp.asarray(sylvester(), jnp.bfloat16)
    vmem = pl.BlockSpec(memory_space=pltpu.VMEM)
    hbm = pl.BlockSpec(memory_space=pl.ANY)
    dma = pltpu.SemaphoreType.DMA
    bf, f32 = jnp.bfloat16, jnp.float32
    shapes = (jax.ShapeDtypeStruct((256, 256), bf), jax.ShapeDtypeStruct((BLOCK, 256), f32))
    raw = pl.pallas_call(
        kernel,
        out_shape=shapes,
        in_specs=[hbm] * 7,
        out_specs=(hbm, hbm),
        scratch_shapes=[
            pltpu.VMEM((2, SHARD), f32),
            pltpu.VMEM((1, 256), jnp.int32),
            pltpu.VMEM((1, 256), jnp.int32),
            pltpu.VMEM((128, 128), bf),
            pltpu.VMEM((SHARD, 256), bf),
            pltpu.VMEM((8, 512, WIN), bf),
            pltpu.VMEM((512, 256), bf),
            pltpu.VMEM((8, WIN, 256), bf),
            pltpu.VMEM((2, 8, WIN, 128), f32),
            pltpu.VMEM((2, 2, 3, 2, HALF, 128), bf),
            pltpu.VMEM((2, 2, 3, 2, HALF, 128), bf),
            pltpu.VMEM((2, 4, HALF + 8, 128), f32),
            pltpu.VMEM((2, 2, 3, 4, 64, 128), bf),
            pltpu.VMEM((2, 2, 3, 4, 64, 128), bf),
            pltpu.VMEM((8, 2, 64, 128), f32),
            pltpu.VMEM((2, 8, 64, 128), bf),
            pltpu.VMEM((2, 7, 64, 128), bf),
            pltpu.VMEM((2, 256, 256), f32),
            pltpu.VMEM((256, 256), f32),
            pltpu.VMEM((256, 256), bf),
            pltpu.VMEM((BLOCK, 256), f32),
            dma((8,)), dma((8,)), dma((8,)), dma((3,)), dma((2,)), dma((4,)),
            dma((9, 2)), dma((8, 2)), dma((8, 2)), dma((8, 2)),
            dma((2, 2, 4)), dma((2, 2, 4)), dma((2, 2, 3)), dma((2, 2, 3)),
            dma((2, 7)), dma((2, 7)), dma((4,)),
        ],
        compiler_params=pltpu.CompilerParams(
            collective_id=0, has_side_effects=True, vmem_limit_bytes=56 * 2**20
        ),
        cost_estimate=pl.CostEstimate(flops=4 * 10**9, bytes_accessed=10**7, transcendentals=0),
    )(
        tokens, cotangent, weight_codes, weight_scales.T,
        weight_bits.reshape(1, 256), grad_bits.reshape(1, 256), table,
    )
    return pl.pallas_call(
        place, out_shape=shapes, in_specs=[vmem, vmem], out_specs=(vmem, vmem)
    )(*raw)


def solution(mesh):
    return jax.shard_map(
        on_device,
        mesh=mesh,
        in_specs=(
            P(("outer", "node"), None),
            P(("outer", "node"), None),
            P("node", None),
            P("node", None),
            P(),
            P(),
        ),
        out_specs=(P(("outer", "node"), None), P(("outer", "node"), None)),
        check_vma=False,
    )
```

```python
import math

import jax
import jax.numpy as jnp
import numpy as np
from jax import lax
from jax.experimental import pallas as pl
from jax.experimental.pallas import tpu as pltpu
from jax.sharding import PartitionSpec as P

MESH = pl.DeviceIdType.MESH
SHARD = 928
BLOCK = 58
WIN = 1024
EDGE = 96
HALF = SHARD // 2
END = 128
RUN = HALF - END
ROOT = 1.0 / math.sqrt(128.0)


def sylvester():
    row_index = np.arange(128).reshape(128, 1)
    column_index = np.arange(128).reshape(1, 128)
    parity = np.zeros((128, 128))
    for level in range(7):
        parity = parity + row_index // 2**level % 2 * (column_index // 2**level % 2)
    return 1.0 - 2.0 * (parity % 2)


def kernel(
    tokens, cot_in, codes, scales_in, wbits_in, gbits_in, table_in,
    out, grad,
    scales, wbits, gbits, table, raw, tok, cot, wts, part, s1, d1, r1, s2, d2, r2, s3, d3, total, other, out_buf, grad_buf,
    tok_loc, tok_ss, tok_rs, cot_sem, code_sem, small_sem, w_ss, w_rs, e_ss, e_rs, ss1, rs1, ss2, rs2, ss3, rs3, o_sem,
):
    o = lax.axis_index("outer")
    n = lax.axis_index("node")
    c = lax.rem(o, 2)
    x = lax.rem(o // 2, 4)
    ylo = o // 8
    yhi = n // 8
    z = lax.rem(n, 8)
    y = yhi * 2 + ylo
    odd = lax.rem(z + c, 2)

    def dev(cc, xx, yy, zz):
        xx, yy, zz = lax.rem(xx + 4, 4), lax.rem(yy + 4, 4), lax.rem(zz + 8, 8)
        return (lax.rem(yy, 2) * 8 + xx * 2 + cc, (yy // 2) * 8 + zz)

    mate = dev(1 - c, x, y, z)
    xp, xm = dev(c, x + 1, y, z), dev(c, x - 1, y, z)
    yp, ym = dev(c, x, y + 1, z), dev(c, x, y - 1, z)
    zp, zm = dev(c, x, y, z + 1), dev(c, x, y, z - 1)
    ypart = dev(c, x, 3 - y, z)
    xodd = lax.rem(x, 2)
    xpair, ypair = dev(c, x + 1 - 2 * xodd, y, z), dev(c, x, y + 1 - 2 * ylo, z)

    small = [
        pltpu.make_async_copy(source, target, small_sem.at[i])
        for i, (source, target) in enumerate(
            ((scales_in, scales), (wbits_in, wbits), (gbits_in, gbits), (table_in, table))
        )
    ]

    def local_codes(i):
        rows = pl.ds(i * HALF, HALF)
        return pltpu.make_async_copy(codes.at[rows], raw.at[rows], code_sem.at[i])

    @pl.when(odd == 0)
    def _():
        local_codes(0).start()
        local_codes(1).start()

    for copy_in in small:
        copy_in.start()

    zero = jnp.zeros((EDGE, 256), jnp.bfloat16)

    @pl.loop(0, 8)
    def _(i):
        wts[i, pl.ds(0, EDGE)] = zero
        wts[i, pl.ds(WIN - EDGE, EDGE)] = zero

    barrier = pltpu.get_barrier_semaphore()
    peers = [mate, xp, xm, yp, ym] + [dev(c, x, y, z + k) for k in range(1, 8)]
    for p in peers:
        pl.semaphore_signal(barrier, inc=1, device_id=p, device_id_type=MESH)

    def start_of(g):
        return pl.multiple_of(g * SHARD - 32 * lax.rem(g, 4), 128)

    def order(i):
        if isinstance(i, int):
            i = jnp.int32(i)
        first = lax.rem(ylo + i, 2) * 4 + lax.rem(x + 2, 4)
        second = ylo * 4 + lax.rem(x + 1 + i, 4)
        third = (1 - ylo) * 4 + lax.rem(x + 2 + i, 4)
        return jnp.where(i < 2, first, jnp.where(i < 5, second, third))

    def local_tok(gi):
        return pltpu.make_async_copy(
            tokens.at[:, pl.ds(start_of(2 * gi + c), WIN)],
            tok.at[gi, pl.ds(pl.multiple_of(c * 256, 256), 256)],
            tok_loc.at[gi],
        )

    def swap_tok(gi):
        return pltpu.make_async_remote_copy(
            src_ref=tokens.at[:, pl.ds(start_of(2 * gi + 1 - c), WIN)],
            dst_ref=tok.at[gi, pl.ds(pl.multiple_of(c * 256, 256), 256)],
            send_sem=tok_ss.at[gi],
            recv_sem=tok_rs.at[gi],
            device_id=mate,
            device_id_type=MESH,
        )

    cot_mine = cot.at[pl.ds(pl.multiple_of(c * 256, 256), 256)]
    local_cot = pltpu.make_async_copy(cot_in, cot_mine, cot_sem.at[0])
    swap_cot = pltpu.make_async_remote_copy(
        src_ref=cot_in, dst_ref=cot_mine, send_sem=cot_sem.at[1], recv_sem=cot_sem.at[2],
        device_id=mate, device_id_type=MESH,
    )
    local_cot.start()

    @pl.loop(0, 8)
    def _(i):
        local_tok(order(i)).start()

    for h in range(2):
        for i in range(4):
            r1[h, i, pl.ds(HALF, 8)] = jnp.zeros((8, 128), jnp.float32)
    total[...] = jnp.zeros_like(total)

    def shard(yy, zz):
        zz = lax.rem(zz + 8, 8)
        slot = yy * 4 + zz // 2
        return slot, 32 * lax.rem(zz, 4)

    def rows_of(yy, zz, first, size):
        slot, base = shard(yy, zz)
        return wts.at[slot, pl.ds(pl.multiple_of(base + first, 16), size)]

    def move(ref, to, ss, rs):
        return pltpu.make_async_remote_copy(
            src_ref=ref, dst_ref=ref, send_sem=ss, recv_sem=rs, device_id=to, device_id_type=MESH
        )

    def push(yy, zz, to, k, i):
        slot, _ = shard(yy, zz)
        skip = (ylo, xodd)[i] * END
        return move(rows_of(yy, zz, i * HALF + skip, RUN), to, w_ss.at[k, i], w_rs.at[slot, i])

    def partner(yy, i):
        slot, _ = shard(yy, z)
        return move(rows_of(yy, z, i * HALF, HALF), ypart, w_ss.at[8, i], w_rs.at[slot, i])

    def swap_end(yy, zz, k, i):
        slot, _ = shard(yy, zz)
        own = (ylo, xodd)[i] * RUN
        return move(rows_of(yy, zz, i * HALF + own, END), (ypair, xpair)[i], e_ss.at[k, i], e_rs.at[slot, i])

    def passing(yy, zz, i, to=None, j=0):
        push(yy, zz, zp, 0, i).wait_recv()
        if to is not None:
            push(yy, zz, to, j, i).start()

    def complete(yy, zz):
        for i in range(2):
            swap_end(yy, zz, 0, i).wait_recv()

    near, far = yhi, 1 - yhi

    def multiply(j, side):
        dz0 = jnp.where(j < 2, 0, jnp.where(j < 6, jnp.where(lax.rem(j, 2) == 0, -2, 2), 4))
        far0 = jnp.where((j == 1) | (j == 4) | (j == 5) | (j == 7), 1, 0)
        dz1 = jnp.where(j < 4, 1, 3) * jnp.where(lax.rem(j, 2) == 0, -1, 1)
        far1 = jnp.where(lax.rem(j, 4) < 2, 0, 1)
        dz = jnp.where(odd == 0, dz0, dz1)
        off = jnp.where(odd == 0, far0, far1)
        slot = lax.rem(yhi + off, 2) * 4 + lax.rem(z + dz + 8, 8) // 2
        rows = pl.ds(pl.multiple_of(lax.rem(c + side, 2) * 256, 256), 256)
        total[side] += jnp.dot(tok[slot, rows], wts[slot], preferred_element_type=jnp.float32)

    def rotate_half(i):
        signs = (2 * wbits[...] - 1).astype(jnp.bfloat16)
        factors = (scales[...] * ROOT).T
        local_codes(i).wait()
        slot, base = shard(near, z)
        lo = i * HALF
        for b in range(2):
            cols = pl.ds(b * 128, 128)
            spun = jnp.dot(
                raw[pl.ds(lo, HALF), cols] * signs[:, b * 128:b * 128 + 128], table[...],
                preferred_element_type=jnp.float32,
            )
            spun = spun * factors[lo:lo + HALF, b:b + 1]
            wts[slot, pl.ds(pl.multiple_of(base + lo, 16), HALF), cols] = spun.astype(jnp.bfloat16)

    for copy_in in small:
        copy_in.wait()

    @pl.when(odd == 0)
    def _():
        rotate_half(0)

    pl.semaphore_wait(barrier, len(peers))

    swap_cot.start()

    def push_own(i):
        push(near, z, zp, 0, i).start()
        push(near, z, zm, 1, i).start()
        partner(near, i).start()

    @pl.when(odd == 0)
    def _():
        push_own(0)

    @pl.loop(0, 2)
    def _(i):
        swap_tok(order(i)).start()

    @pl.when(odd == 0)
    def _():
        rotate_half(1)
        push_own(1)

    @pl.loop(2, 8)
    def _(i):
        swap_tok(order(i)).start()

    local_cot.wait()
    swap_cot.wait_recv()

    def produce(i):
        gi = order(i)
        local_tok(gi).wait()
        swap_tok(gi).wait_recv()
        sums = lax.dot_general(
            tok[gi], cot[...], (((0,), (0,)), ((), ())), preferred_element_type=jnp.float32
        )
        part[0, gi] = sums[:, :128]
        part[1, gi] = sums[:, 128:]

    def ring(level, h):
        along_x = (h == 0) == (level == 1)
        pos = x if along_x else y
        ends = (xp, xm) if along_x else (yp, ym)
        sent, got = (s1, d1) if level == 1 else (s2, d2)
        ssem, rsem = (ss1, rs1) if level == 1 else (ss2, rs2)
        total = r1 if level == 1 else r2

        def copy(way, m, piece=None):
            place_of = (h, way, m) if piece is None else (h, way, 2, piece)
            return pltpu.make_async_remote_copy(
                src_ref=sent.at[place_of], dst_ref=got.at[place_of],
                send_sem=ssem.at[h, way, m], recv_sem=rsem.at[h, way, m],
                device_id=ends[way], device_id_type=MESH,
            )

        count = 2 if level == 1 else 4
        first = 1 - yhi if h == 0 else 0
        turn = (first, 1 - first)

        def read(dest, half, i):
            if level == 1:
                gi = half * 4 + dest if h == 0 else lax.rem(dest, 2) * 4 + lax.rem(x + 2 + 2 * half + i, 4)
                top = 32 * lax.rem(2 * gi + c, 4) + (i if h == 0 else dest // 2) * HALF
                return part[h, gi, pl.ds(pl.multiple_of(top, 16), HALF)]
            block = lax.rem(dest, 2) * 2 + dest // 2 if h == 0 else lax.rem(dest - x + 6, 4)
            return r1[h, block, pl.ds(BLOCK * (half * 4 + i), 64)]

        def send(way, m):
            off = (2, 1, 1)[m] if way == 0 else (2, 3, 3)[m]
            dest = lax.rem(pos + off, 4)
            half = (0, 1, 0)[m] if way == 0 else (1, 0, 1)[m]
            if m == 2:
                copy(way, 0).wait_recv()
            for j in range(count):
                i = turn[j] if level == 1 and m == 2 else j
                value = read(dest, half, i)
                if m == 2:
                    value = value + got[h, way, 0, i].astype(jnp.float32)
                sent[h, way, m, i] = value.astype(jnp.bfloat16)
                if level == 1 and m == 2:
                    copy(way, 2 + j, i).start()
            if level == 2 or m < 2:
                copy(way, m).start()

        def finish(j=0):
            for half in range(2):
                a, b = ((0, 2), (1, 1)) if half == 0 else ((0, 1), (1, 2))
                for way, m in (b, a):
                    if level == 1 and m == 2:
                        copy(way, 2 + j, turn[j]).wait_recv()
                    elif j == 0:
                        copy(way, m).wait_recv()
                for i in ((turn[j],) if level == 1 else range(count)):
                    value = (
                        read(pos, half, i)
                        + got[(h,) + a + (i,)].astype(jnp.float32)
                        + got[(h,) + b + (i,)].astype(jnp.float32)
                    )
                    if level == 1:
                        r1[h, half * 2 + i, pl.ds(0, HALF)] = value
                    else:
                        r2[half * 4 + i, h] = value

        def drain():
            for way in range(2):
                for m in range(4 if level == 1 else 3):
                    copy(way, m, turn[m - 2] if level == 1 and m > 1 else None).wait_send()

        return send, finish, drain

    send_a, finish_a, drain_a = ring(1, 0)
    send_b, finish_b, drain_b = ring(1, 1)
    send_c, finish_c, drain_c = ring(2, 0)
    send_d, finish_d, drain_d = ring(2, 1)

    def last(h, k):
        to = lax.rem(z + k, 8)
        return pltpu.make_async_remote_copy(
            src_ref=s3.at[h, to], dst_ref=d3.at[h, k - 1],
            send_sem=ss3.at[h, k - 1], recv_sem=rs3.at[h, k - 1],
            device_id=dev(c, x, y, z + k), device_id_type=MESH,
        )

    def last_sends(h):
        for i in range(8):
            s3[h, i] = r2[i, h].astype(jnp.bfloat16)
        for k in (4, 3, 5, 2, 6, 1, 7):
            last(h, k).start()

    def far_own(i):
        partner(far, i).wait_recv()
        push(far, z, zp, 2, i).start()
        push(far, z, zm, 3, i).start()

    def pass_pair(yy, d, i, first, second):
        passing(yy, z - d, i, *first)
        passing(yy, z + d, i, *second)

    def ends(yy, d, k, i):
        swap_end(yy, z - d, k, i).start()
        swap_end(yy, z + d, k + 1, i).start()

    def both(yy, d):
        complete(yy, z - d)
        complete(yy, z + d)

    def ring_start(send, *ms):
        for m in ms:
            send(0, m)
            send(1, m)

    def product(first, last_one, *sides):
        for side in sides:
            pl.loop(first, last_one)(lambda j: multiply(j, side))

    def run(who, act):
        if who == 2:
            act()
        else:
            pl.when(odd == who)(act)

    swap_out = pltpu.make_async_remote_copy(
        src_ref=total.at[1], dst_ref=other, send_sem=o_sem.at[0], recv_sem=o_sem.at[1],
        device_id=mate, device_id_type=MESH,
    )
    write_out = pltpu.make_async_copy(out_buf, out, o_sem.at[2])
    write_grad = pltpu.make_async_copy(grad_buf, grad, o_sem.at[3])

    steps = [
        (2.5, 2, lambda: pl.loop(0, 2)(produce)),
        (2.6, 2, lambda: ring_start(send_a, 0)),
        (3.3, 1, lambda: pass_pair(near, 1, 0, (zp, 0), (zm, 1))),
        (3.33, 1, lambda: ends(near, 1, 0, 0)),
        (4.5, 2, lambda: pl.loop(2, 3)(produce)),
        (5.4, 1, lambda: pass_pair(near, 1, 1, (zp, 0), (zm, 1))),
        (5.43, 1, lambda: ends(near, 1, 0, 1)),
        (5.98, 2, lambda: send_b(0, 0)),
        (6.0, 2, lambda: pl.loop(3, 5)(produce)),
        (6.1, 2, lambda: send_b(1, 0)),
        (6.78, 0, lambda: far_own(0)),
        (7.0, 1, lambda: pass_pair(far, 1, 0, (zp, 2), (zm, 3))),
        (7.03, 1, lambda: ends(far, 1, 2, 0)),
        (8.78, 0, lambda: far_own(1)),
        (9.0, 2, lambda: pl.loop(5, 8)(produce)),
        (9.01, 1, lambda: pass_pair(far, 1, 1, (zp, 2), (zm, 3))),
        (9.03, 1, lambda: ends(far, 1, 2, 1)),
        (9.1, 2, lambda: ring_start(send_a, 1)),
        (9.2, 2, lambda: ring_start(send_b, 1)),
        (10.5, 2, lambda: ring_start(send_a, 2)),
        (10.78, 0, lambda: pass_pair(near, 2, 0, (zp, 4), (zm, 5))),
        (10.8, 0, lambda: ends(near, 2, 0, 0)),
        (12.78, 0, lambda: pass_pair(near, 2, 1, (zp, 4), (zm, 5))),
        (12.8, 0, lambda: ends(near, 2, 0, 1)),
        (13.5, 2, lambda: ring_start(send_b, 2)),
        (14.1, 1, lambda: pass_pair(near, 3, 0, (zp, 4), ())),
        (14.13, 1, lambda: ends(near, 3, 4, 0)),
        (14.88, 0, lambda: pass_pair(far, 2, 0, (zp, 6), (zm, 7))),
        (14.9, 0, lambda: ends(far, 2, 2, 0)),
        (15.7, 1, lambda: both(far, 1)),
        (16.0, 1, lambda: pass_pair(near, 3, 1, (zp, 4), ())),
        (16.03, 1, lambda: ends(near, 3, 4, 1)),
        (16.78, 0, lambda: pass_pair(far, 2, 1, (zp, 6), (zm, 7))),
        (16.8, 0, lambda: ends(far, 2, 2, 1)),
        (16.81, 1, lambda: both(near, 1)),
        (16.9, 0, lambda: both(near, 2)),
        (17.0, 2, lambda: product(0, 4, 1, 0)),
        (19.5, 2, finish_a),
        (19.6, 2, lambda: ring_start(send_c, 0)),
        (20.5, 2, lambda: finish_a(1)),
        (20.6, 2, lambda: ring_start(send_c, 1)),
        (21.5, 2, finish_b),
        (21.6, 2, lambda: ring_start(send_d, 0)),
        (21.78, 0, lambda: passing(near, z + 4, 0)),
        (21.8, 0, lambda: swap_end(near, z + 4, 4, 0).start()),
        (21.9, 1, lambda: pass_pair(far, 3, 1, (), (zm, 5))),
        (21.93, 1, lambda: ends(far, 3, 6, 1)),
        (22.02, 1, lambda: pass_pair(far, 3, 0, (), (zm, 5))),
        (22.04, 1, lambda: ends(far, 3, 6, 0)),
        (22.4, 2, lambda: ring_start(send_c, 2)),
        (23.0, 2, lambda: finish_b(1)),
        (23.1, 2, lambda: ring_start(send_d, 1)),
        (24.28, 0, lambda: passing(near, z + 4, 1)),
        (24.3, 0, lambda: swap_end(near, z + 4, 4, 1).start()),
        (24.5, 2, lambda: ring_start(send_d, 2)),
        (24.9, 0, lambda: both(far, 2)),
        (24.91, 1, lambda: both(near, 3)),
        (25.0, 2, lambda: product(4, 6, 1, 0)),
        (25.5, 2, finish_c),
        (25.52, 2, lambda: last_sends(0)),
        (28.2, 0, lambda: passing(far, z + 4, 0)),
        (28.22, 0, lambda: swap_end(far, z + 4, 5, 0).start()),
        (28.5, 2, finish_d),
        (28.6, 2, lambda: last_sends(1)),
        (30.66, 0, lambda: passing(far, z + 4, 1)),
        (30.68, 0, lambda: swap_end(far, z + 4, 5, 1).start()),
        (35.8, 0, lambda: complete(near, z + 4)),
        (35.9, 0, lambda: complete(far, z + 4)),
        (35.91, 1, lambda: both(far, 3)),
        (36.0, 2, lambda: product(6, 8, 1)),
        (36.1, 2, lambda: swap_out.start()),
        (38.95, 2, lambda: product(6, 8, 0)),
    ]
    for _, who, act in sorted(steps, key=lambda step: step[0]):
        run(who, act)

    gsigns = (2 * gbits[...] - 1).astype(jnp.float32)
    for h in range(2):
        value = r2[z, h]
        for k in range(1, 8):
            last(h, k).wait_recv()
            value = value + d3[h, k - 1].astype(jnp.float32)
        value = value * gsigns[:, h * 128:h * 128 + 128]
        spun = jnp.zeros((64, 128), jnp.float32)
        for _ in range(3):
            head = value.astype(jnp.bfloat16)
            spun = spun + jnp.dot(head, table[...], preferred_element_type=jnp.float32)
            value = value - head.astype(jnp.float32)
        grad_buf[:, h * 128:h * 128 + 128] = (spun * ROOT)[:BLOCK]
    write_grad.start()

    swap_out.wait_recv()
    out_buf[...] = (total[0] + other[...]).astype(jnp.bfloat16)
    write_out.start()

    swap_out.wait_send()
    swap_cot.wait_send()

    @pl.loop(0, 8)
    def _(i):
        swap_tok(i).wait_send()

    drain_a()
    drain_b()
    drain_c()
    drain_d()
    for h in range(2):
        for k in range(1, 8):
            last(h, k).wait_send()

    def sent_all(pushes, ends):
        for i in range(2):
            for k in range(pushes):
                push(near, z + odd, zp, k, i).wait_send()
            for k in range(ends):
                swap_end(near, z + odd, k, i).wait_send()

    def sent_even():
        for i in range(2):
            partner(near, i).wait_send()
        sent_all(8, 6)

    run(0, sent_even)
    run(1, lambda: sent_all(6, 8))
    write_grad.wait()
    write_out.wait()


def place(out_in, grad_in, out, grad):
    out[...] = out_in[...]
    grad[...] = grad_in[...]


def on_device(tokens, cotangent, weight_codes, weight_scales, weight_bits, grad_bits):
    table = jnp.asarray(sylvester(), jnp.bfloat16)
    vmem = pl.BlockSpec(memory_space=pltpu.VMEM)
    hbm = pl.BlockSpec(memory_space=pl.ANY)
    dma = pltpu.SemaphoreType.DMA
    bf, f32 = jnp.bfloat16, jnp.float32
    shapes = (jax.ShapeDtypeStruct((256, 256), bf), jax.ShapeDtypeStruct((BLOCK, 256), f32))
    raw = pl.pallas_call(
        kernel,
        out_shape=shapes,
        in_specs=[hbm] * 7,
        out_specs=(hbm, hbm),
        scratch_shapes=[
            pltpu.VMEM((2, SHARD), f32),
            pltpu.VMEM((1, 256), jnp.int32),
            pltpu.VMEM((1, 256), jnp.int32),
            pltpu.VMEM((128, 128), bf),
            pltpu.VMEM((SHARD, 256), bf),
            pltpu.VMEM((8, 512, WIN), bf),
            pltpu.VMEM((512, 256), bf),
            pltpu.VMEM((8, WIN, 256), bf),
            pltpu.VMEM((2, 8, WIN, 128), f32),
            pltpu.VMEM((2, 2, 3, 2, HALF, 128), bf),
            pltpu.VMEM((2, 2, 3, 2, HALF, 128), bf),
            pltpu.VMEM((2, 4, HALF + 8, 128), f32),
            pltpu.VMEM((2, 2, 3, 4, 64, 128), bf),
            pltpu.VMEM((2, 2, 3, 4, 64, 128), bf),
            pltpu.VMEM((8, 2, 64, 128), f32),
            pltpu.VMEM((2, 8, 64, 128), bf),
            pltpu.VMEM((2, 7, 64, 128), bf),
            pltpu.VMEM((2, 256, 256), f32),
            pltpu.VMEM((256, 256), f32),
            pltpu.VMEM((256, 256), bf),
            pltpu.VMEM((BLOCK, 256), f32),
            dma((8,)), dma((8,)), dma((8,)), dma((3,)), dma((2,)), dma((4,)),
            dma((9, 2)), dma((8, 2)), dma((8, 2)), dma((8, 2)),
            dma((2, 2, 4)), dma((2, 2, 4)), dma((2, 2, 3)), dma((2, 2, 3)),
            dma((2, 7)), dma((2, 7)), dma((4,)),
        ],
        compiler_params=pltpu.CompilerParams(
            collective_id=0, has_side_effects=True, vmem_limit_bytes=56 * 2**20
        ),
        cost_estimate=pl.CostEstimate(flops=4 * 10**9, bytes_accessed=10**7, transcendentals=0),
    )(
        tokens, cotangent, weight_codes, weight_scales.T,
        weight_bits.reshape(1, 256), grad_bits.reshape(1, 256), table,
    )
    return pl.pallas_call(
        place, out_shape=shapes, in_specs=[vmem, vmem], out_specs=(vmem, vmem)
    )(*raw)


def solution(mesh):
    return jax.shard_map(
        on_device,
        mesh=mesh,
        in_specs=(
            P(("outer", "node"), None),
            P(("outer", "node"), None),
            P("node", None),
            P("node", None),
            P(),
            P(),
        ),
        out_specs=(P(("outer", "node"), None), P(("outer", "node"), None)),
        check_vma=False,
    )
```
